128 devices in a mesh: shot: 16 (over y, x_hi, core), pt: 8 (over z, x_lo).
Axes of the slice: x: 4 (x_hi: 2, x_lo: 2; x = x_hi * 2 + x_lo), y: 4, z: 4, core: 2. Of those that a mesh axis runs over, the one named last changes fastest.
Arguments:
- shot_data: bfloat16 [256, 128, 1024], P('shot', 'pt'), may hold values from -0.29882812 to 0.29882812
- point_store: bfloat16 [128, 576, 1024], P(('shot', 'pt')), may hold values from -0.29882812 to 0.29882812
- point_slot: int32 [128], P('pt'), may hold values from 0 to 127, as said below
- taper_mask: int32 [256, 128], P('shot', 'pt'), may hold values 0 or 1
- recv_start: int32 [256], P('shot'), may hold values from 0 to 64
Outputs:
- multiples: float32 [256, 512, 1024], P('shot', 'pt')
The draws below stay inside these ranges and needn't reach their ends.
Inputs may be any that keep to these rules, and one draw needn't show every extreme that they name: `point_slot`: A permutation of the slots; the gathers of the inner points k with k // 16 = b lie in the slots q with (q) % (8) = b.
All inputs are finite; a program needn't handle non-finite values. No bound on the sum of `taper_mask` on one device may be relied on, other than what follows from the above.
Results may differ from the reference program's by a relative error of at most 0.0063.
Values may be sent and summed in bfloat16 or wider, within the bound.
No kernel may reach another device: no remote copies, remote signals or barrier semaphores. Data moves between devices by JAX's collectives and lax.ppermute only.
A program may use at most 192 MiB of HBM per device.

```python
import math
import jax
import jax.numpy as jnp
from jax import lax

INNER_DEV = 16
NT = 1024
NF = 256
SPREAD = 512
SHIFT = 64
GRID = 576
SHOTS = 256
INNER = 128
OWN = 1


def draw_point_slot(key, part):
    key = jax.random.fold_in(key, 7)
    groups = INNER // INNER_DEV
    keys = jax.random.split(key, groups)
    perms = jax.vmap(lambda each_key: jax.random.permutation(each_key, INNER_DEV))(keys).astype(jnp.int32)
    group_idx = jnp.arange(groups, dtype=jnp.int32)[:, None]
    owner = perms // OWN
    within = perms % OWN
    slots = (owner * groups + group_idx) * OWN + within
    return slots.reshape(INNER).astype(jnp.int32)


def place_ends(drawn, key, least, largest):
    index_at = [jax.random.randint(jax.random.fold_in(key, axis), (), 0, length) for axis, length in enumerate(drawn.shape)]
    longest = drawn.shape.index(max(drawn.shape))
    neighbour = index_at[:longest] + [(index_at[longest] + 1) % drawn.shape[longest]] + index_at[longest + 1:]
    return drawn.at[tuple(index_at)].set(least).at[tuple(neighbour)].set(largest)


def steps_of(rng, shape, cuts, least, high):
    def one(position, shards_of):
        heights = jax.random.uniform(jax.random.fold_in(jax.random.fold_in(rng, 6), position), (shards_of,), jnp.float32, least / len(cuts), high / len(cuts))
        return jnp.repeat(jnp.exp(heights), shape[position] // shards_of).reshape((-1,) + (1,) * (len(shape) - position - 1))

    level = one(*cuts[0])
    for cut in cuts[1:]:
        level = level * one(*cut)
    return level


def scatter_about(own_key, shape, scale, most, pieces=(), kind=jnp.bfloat16):
    entries = jax.random.normal(own_key, shape, jnp.float32) * scale
    if len(pieces) > 0:
        entries = steps_of(own_key, shape, pieces, -0.22, 0.18) * entries
    return jnp.clip(entries, min=-most, max=most).astype(kind)


def setup_inputs(seed: int = 0) -> dict:
    seeds = jax.random.split(jax.random.key(seed), 6)
    shot_data = scatter_about(seeds[0], (SHOTS, INNER, NT), 0.05, 0.29882812, ((0, 16), (1, 8)))
    point_store = scatter_about(seeds[1], (INNER, GRID, NT), 0.05, 0.29882812, ((0, 128),))
    point_slot = draw_point_slot(jax.random.fold_in(seeds[5], 71), 0)
    taper_mask = place_ends((jax.random.randint(seeds[3], (SHOTS, INNER), 0, 4) < 3).astype(jnp.int32), jax.random.fold_in(seeds[3], 1), 0, 1)
    recv_start = place_ends(jax.random.randint(seeds[4], (SHOTS,), 0, SHIFT + 1), jax.random.fold_in(seeds[4], 1), 0, SHIFT).astype(jnp.int32)
    return dict(shot_data=shot_data, point_store=point_store, point_slot=point_slot, taper_mask=taper_mask, recv_start=recv_start)


def band_tables(samples, bins):
    times_idx = jnp.arange(samples, dtype=jnp.int32)[:, None]
    freq_idx = jnp.arange(bins, dtype=jnp.int32)[None, :]
    phase_idx = (times_idx * freq_idx) % samples
    phase_angle = phase_idx.astype(jnp.float32) * jnp.float32(2.0 * math.pi / samples)
    cosine = jnp.cos(phase_angle)
    sine = jnp.sin(phase_angle)
    forward = jnp.concatenate([cosine, -sine], axis=1).astype(jnp.bfloat16)
    weights = jnp.where(freq_idx == 0, jnp.float32(1.0), jnp.float32(2.0)) / jnp.float32(samples)
    inverse = jnp.concatenate([(weights * cosine).T, (-weights * sine).T], axis=0).astype(jnp.bfloat16)
    return forward, inverse


def complex_product(left_part, right_part, bins):
    left_real = left_part[..., :bins].astype(jnp.float32)
    left_imag = left_part[..., bins:].astype(jnp.float32)
    right_real = right_part[..., :bins].astype(jnp.float32)
    right_imag = right_part[..., bins:].astype(jnp.float32)
    real_part = jnp.einsum("skf,krf->srf", left_real, right_real) - jnp.einsum("skf,krf->srf", left_imag, right_imag)
    imag_part = jnp.einsum("skf,krf->srf", left_real, right_imag) + jnp.einsum("skf,krf->srf", left_imag, right_real)
    return jnp.concatenate([real_part, imag_part], axis=-1)


def reference(shot_data, point_store, point_slot, taper_mask, recv_start):
    forward, inverse = band_tables(NT, NF)
    spectra = jnp.dot(shot_data, forward, preferred_element_type=jnp.float32)
    spectra = (spectra * taper_mask[:, :, None].astype(jnp.float32)).astype(jnp.bfloat16)
    store_spec = jnp.dot(point_store, forward, preferred_element_type=jnp.float32).astype(jnp.bfloat16)
    gathers = jnp.take(store_spec, point_slot.astype(jnp.int32), axis=0)
    predicted = complex_product(spectra, gathers, NF)

    def window(shot_row, first_rec):
        return lax.dynamic_slice_in_dim(shot_row, first_rec.astype(jnp.int32), SPREAD, 0)

    windows = jax.vmap(window)(predicted, recv_start).astype(jnp.bfloat16)
    return jnp.dot(windows, inverse, preferred_element_type=jnp.float32)
```

```python
import functools
import math

import jax
import jax.numpy as jnp
import numpy as np
from jax import lax
from jax.experimental import pallas as pl
from jax.experimental.pallas import tpu as pltpu
from jax.sharding import PartitionSpec as P


NT = 1024
NF = 256
GRID = 576
SPREAD = 512
DEV = 128
ROWS = 4
NS = 16
NPT = 8
SHARE = 64
VMEM = 56 * 1024 * 1024


def band_tables():
    phase = (np.arange(NT)[:, None] * np.arange(NF)[None, :]) % NT
    angle = phase.astype(np.float32) * np.float32(2.0 * math.pi / NT)
    cosine = np.cos(angle).T
    sine = np.sin(angle).T
    weights = np.where(np.arange(NF) == 0, 1.0, 2.0).astype(np.float32)[:, None] / np.float32(NT)
    forward = np.stack([cosine[0::2], -sine[0::2], cosine[1::2], -sine[1::2]])
    wc, ws = weights * cosine, -weights * sine
    inverse = np.stack([wc[0::2], ws[0::2], wc[1::2], ws[1::2]])
    forward = jnp.asarray(forward.reshape(ROWS * DEV, NT), jnp.bfloat16)
    inverse = jnp.asarray(inverse.reshape(ROWS * DEV, NT), jnp.bfloat16)
    return forward, inverse


def iota(shape, dim):
    return lax.broadcasted_iota(jnp.int32, shape, dim)


def dot_nt(left, right):
    return lax.dot_general(left, right, (((1,), (1,)), ((), ())), preferred_element_type=jnp.float32)


def dot_nn(left, right):
    return jnp.dot(left, right, preferred_element_type=jnp.float32)


def forward_kernel(shot_ref, store_ref, slot_ref, mask_ref, start_ref, table_ref, out_ref, rows):
    f32, b16 = jnp.float32, jnp.bfloat16
    wide = NS * NS
    spread = (iota((NS, wide), 1) % NS == iota((NS, wide), 0)).astype(f32).astype(b16)
    owner = lax.shift_right_logical(slot_ref[...], 3).astype(f32).astype(b16)
    owner = dot_nn(jnp.broadcast_to(owner, (NS, NS)), spread)[0:1].astype(jnp.int32)
    taper = dot_nn(mask_ref[...].astype(f32).astype(b16), spread)
    taper = jnp.where(iota((NS, wide), 1) // NS == iota((NS, wide), 0), taper, 0.0)
    taper = jnp.sum(taper, axis=0, keepdims=True)
    r, l = iota((wide, wide), 0), iota((wide, wide), 1)
    order = jnp.where((r // NS == l // NS) & (owner == r % NS), taper, 0.0).astype(b16)
    table = table_ref[...]
    spectra = dot_nt(table, shot_ref[...].reshape(wide, NT)).astype(b16)
    ordered = dot_nt(spectra, order)
    gathers = dot_nt(table, store_ref[0, 0:SPREAD])
    tail = jnp.concatenate([store_ref[0, SPREAD:GRID], jnp.zeros((64, NT), b16)], axis=0)
    tail = dot_nt(table, tail)
    pick = (iota((NS, 128), 1) - 64 == iota((NS, 128), 0)).astype(f32).astype(b16)
    start = start_ref[...].astype(f32).astype(b16)
    start = dot_nn(jnp.broadcast_to(start, (NS, NS)), pick)[0:1]
    tail = tail + start
    for block, value in ((0, ordered), (2, gathers), (6, tail)):
        for n in range(value.shape[1] // 128):
            for c in range(ROWS):
                rows[pl.ds(4 * (block + n) + c, DEV, 32), :] = value[c * DEV : (c + 1) * DEV, 128 * n : 128 * (n + 1)]
    for c in range(ROWS):
        rows[pl.ds(28 + c, DEV, 32), :] = jnp.zeros((DEV, 128), f32)
    out_ref[...] = rows[...].astype(b16).reshape(DEV, 32, 128)


def product_kernel(in_ref, out_ref, rows, left, prod, wins):
    f32, b16 = jnp.float32, jnp.bfloat16
    rows[...] = in_ref[...].reshape(DEV * 32, 128).astype(f32)

    def piece(block, c):
        return rows[pl.ds(4 * block + c, DEV, 32), :]

    a, b = iota((128, 1024), 0), iota((128, 1024), 1)
    tile = ((a // 16 == b // 128) & (a % 16 == (b % 128) // 8)).astype(f32).astype(b16)
    halves = []
    keep = iota((512, 1024), 0) % 8 == iota((512, 1024), 1) % 8
    fold = (iota((64, 512), 0) == iota((64, 512), 1) // 8).astype(f32).astype(b16)
    for half in range(2):
        arrived = jnp.concatenate([piece(half, c) for c in range(ROWS)], axis=0).astype(b16)
        spread = dot_nn(arrived, tile)
        spread = jnp.where(keep, spread, 0.0).astype(b16)
        halves.append(dot_nn(fold, spread))
    for f in range(2):
        for s in range(NS):
            part = halves[s // 8][:, (s % 8) * 128 : (s % 8 + 1) * 128]
            re = part[(2 * f) * NS : (2 * f + 1) * NS]
            im = part[(2 * f + 1) * NS : (2 * f + 2) * NS]
            left[s * NS : (s + 1) * NS, 0:128] = re.astype(b16)
            left[s * NS : (s + 1) * NS, 128:256] = (-im).astype(b16)
            left[256 + s * NS : 256 + (s + 1) * NS, 0:128] = im.astype(b16)
            left[256 + s * NS : 256 + (s + 1) * NS, 128:256] = re.astype(b16)
        for n in range(5):
            right = jnp.concatenate([piece(2 + n, 2 * f), piece(2 + n, 2 * f + 1)], axis=0).astype(b16)
            prod[f * 512 : (f + 1) * 512, 128 * n : 128 * (n + 1)] = dot_nn(left[...], right)
    first = rows[pl.ds(24, NS, 32 * NPT), :][:, 64:80]
    lane = iota((NS, 128), 1)
    low = lane < 64
    for pair in range(NS // 2):
        begin = [
            jnp.broadcast_to(first[:, 2 * pair + e : 2 * pair + e + 1], (NS, 128)).astype(jnp.int32) for e in range(2)
        ]
        at = [lane + begin[0], lane + begin[1] + 64]
        index = [x & 127 for x in at]
        other = [(x + 64) & 127 for x in at]
        here = [lane + begin[0] + 64 < 128, lane + begin[1] < 128]
        for c in range(ROWS):
            base = c * 256 + 2 * pair * NS
            ahead = [None, None]
            for v in range(4, -1, -1):
                even, odd = [], []
                for e in range(2):
                    src = prod[base + e * NS : base + (e + 1) * NS, 128 * v : 128 * (v + 1)]
                    turned = jnp.take_along_axis(src, other[e], axis=1)
                    if v < 4:
                        even.append(jnp.take_along_axis(src, index[e], axis=1))
                        odd.append(jnp.where(here[e], turned, ahead[e]))
                    ahead[e] = turned
                if v < 4:
                    slot = c * 8 + pair
                    wins[pl.ds(2 * v * 32 + slot, NS, 256), :] = jnp.where(low, even[0], even[1])
                    wins[pl.ds((2 * v + 1) * 32 + slot, NS, 256), :] = jnp.where(low, odd[0], odd[1])
    out_ref[...] = wins[...].astype(b16).reshape(DEV, 32, 128)


def inverse_kernel(in_ref, table_ref, out_ref, rows):
    step = pl.program_id(0)

    @pl.when(step == 0)
    def _():
        rows[...] = in_ref[...].reshape(DEV * 32, 128).astype(jnp.float32)

    parts = [rows[pl.ds(c * 8 + step, DEV, 32), :].T for c in range(ROWS)]
    left = jnp.concatenate(parts, axis=1).astype(jnp.bfloat16)
    out_ref[...] = dot_nn(left, table_ref[...]).reshape(2, SHARE, NT)


def per_device(shot_data, point_store, point_slot, taper_mask, recv_start):
    forward, inverse = band_tables()
    params = pltpu.CompilerParams(vmem_limit_bytes=VMEM)
    sent = pl.pallas_call(
        forward_kernel,
        out_shape=jax.ShapeDtypeStruct((DEV, 32, 128), jnp.bfloat16),
        scratch_shapes=[pltpu.VMEM((DEV * 32, 128), jnp.float32)],
        compiler_params=params,
        name="forward",
    )(shot_data, point_store, point_slot.reshape(1, NS), taper_mask, recv_start.reshape(1, NS), forward)
    got = lax.all_to_all(sent, ("shot", "pt"), 0, 0, tiled=True)
    windows = pl.pallas_call(
        product_kernel,
        out_shape=jax.ShapeDtypeStruct((DEV, 32, 128), jnp.bfloat16),
        scratch_shapes=[
            pltpu.VMEM((DEV * 32, 128), jnp.float32),
            pltpu.VMEM((512, 256), jnp.bfloat16),
            pltpu.VMEM((1024, 640), jnp.float32),
            pltpu.VMEM((DEV * 32, 128), jnp.float32),
        ],
        compiler_params=params,
        name="product",
    )(got)
    back = lax.all_to_all(windows, ("shot", "pt"), 0, 0, tiled=True)
    return pl.pallas_call(
        inverse_kernel,
        grid=(NS // 2,),
        in_specs=[
            pl.BlockSpec((DEV, 32, 128), lambda i: (0, 0, 0)),
            pl.BlockSpec((ROWS * DEV, NT), lambda i: (0, 0)),
        ],
        out_specs=pl.BlockSpec((2, SHARE, NT), lambda i: (i, 0, 0)),
        out_shape=jax.ShapeDtypeStruct((NS, SHARE, NT), jnp.float32),
        scratch_shapes=[pltpu.VMEM((DEV * 32, 128), jnp.float32)],
        compiler_params=params,
        name="inverse",
    )(back, inverse)


def solution(mesh):
    placed = (
        P("shot", "pt", None),
        P(("shot", "pt"), None, None),
        P("pt"),
        P("shot", "pt"),
        P("shot"),
    )
    return jax.shard_map(
        per_device, mesh=mesh, in_specs=placed, out_specs=P("shot", "pt", None), check_vma=False
    )
```

```python
import functools
import math

import jax
import jax.numpy as jnp
import numpy as np
from jax import lax
from jax.experimental import pallas as pl
from jax.experimental.pallas import tpu as pltpu
from jax.sharding import PartitionSpec as P


NT = 1024
NF = 256
GRID = 576
SPREAD = 512
DEV = 128
ROWS = 4
NS = 16
NPT = 8
SHARE = 64
VMEM = 56 * 1024 * 1024
BLOCKS = 8
PITCH = 40


def band_tables():
    phase = (np.arange(NT)[:, None] * np.arange(NF)[None, :]) % NT
    angle = phase.astype(np.float32) * np.float32(2.0 * math.pi / NT)
    cosine = np.cos(angle).T
    sine = np.sin(angle).T
    weights = np.where(np.arange(NF) == 0, 1.0, 2.0).astype(np.float32)[:, None] / np.float32(NT)
    forward = np.stack([cosine[0::2], -sine[0::2], cosine[1::2], -sine[1::2]])
    wc, ws = weights * cosine, -weights * sine
    inverse = np.stack([wc[0::2], ws[0::2], wc[1::2], ws[1::2]])
    forward = jnp.asarray(forward.reshape(ROWS * DEV, NT), jnp.bfloat16)
    inverse = jnp.asarray(inverse.reshape(ROWS * DEV, NT), jnp.bfloat16)
    return forward, inverse


def iota(shape, dim):
    return lax.broadcasted_iota(jnp.int32, shape, dim)


def dot_nt(left, right):
    return lax.dot_general(left, right, (((1,), (1,)), ((), ())), preferred_element_type=jnp.float32)


def dot_nn(left, right):
    return jnp.dot(left, right, preferred_element_type=jnp.float32)


def unpack(in_ref, rows):
    for d in range(DEV):
        rows[d * PITCH : d * PITCH + 32] = in_ref[d].astype(jnp.float32)


def order_matrix(slot_ref, mask_ref):
    f32, b16 = jnp.float32, jnp.bfloat16
    wide = NS * NS
    spread = (iota((NS, wide), 1) % NS == iota((NS, wide), 0)).astype(f32).astype(b16)
    owner = lax.shift_right_logical(slot_ref[...], 3).astype(f32).astype(b16)
    owner = dot_nn(jnp.broadcast_to(owner, (NS, NS)), spread)[0:1].astype(jnp.int32)
    taper = dot_nn(mask_ref[...].astype(f32).astype(b16), spread)
    taper = jnp.where(iota((NS, wide), 1) // NS == iota((NS, wide), 0), taper, 0.0)
    taper = jnp.sum(taper, axis=0, keepdims=True)
    r, l = iota((wide, wide), 0), iota((wide, wide), 1)
    return jnp.where((r // NS == l // NS) & (owner == r % NS), taper, 0.0).astype(b16)


def forward_kernel(shot_any, store_any, slot_ref, mask_ref, start_ref, table_any, out_ref, shot, store, table, rows, sems):
    f32, b16 = jnp.float32, jnp.bfloat16
    load_shot = pltpu.make_async_copy(shot_any, shot, sems.at[0])
    load_table = pltpu.make_async_copy(table_any, table, sems.at[1])
    load_store = pltpu.make_async_copy(store_any.at[0], store, sems.at[2])
    load_shot.start()
    load_table.start()
    load_store.start()
    order = order_matrix(slot_ref, mask_ref)
    pick = (iota((NS, 128), 1) - 64 == iota((NS, 128), 0)).astype(f32).astype(b16)
    start = start_ref[...].astype(f32).astype(b16)
    start = dot_nn(jnp.broadcast_to(start, (NS, NS)), pick)[0:1]
    for c in range(ROWS):
        rows[pl.ds(28 + c, DEV, PITCH), :] = jnp.zeros((DEV, 128), f32)

    def put(block, value):
        for n in range(value.shape[1] // 128):
            for c in range(ROWS):
                rows[pl.ds(4 * (block + n) + c, DEV, PITCH), :] = value[c * DEV : (c + 1) * DEV, 128 * n : 128 * (n + 1)]

    load_shot.wait()
    load_table.wait()
    spectra = dot_nt(table[...], shot[...].reshape(NS * NS, NT)).astype(b16)
    put(0, dot_nt(spectra, order))
    load_store.wait()
    for h in range(2):
        put(2 + 2 * h, dot_nt(table[...], store[256 * h : 256 * (h + 1)]))
    tail = jnp.concatenate([store[SPREAD:GRID], jnp.zeros((64, NT), b16)], axis=0)
    put(6, dot_nt(table[...], tail) + start)
    for d in range(DEV):
        out_ref[d] = rows[d * PITCH : d * PITCH + 32].astype(b16)


def product_kernel(in_ref, out_ref, rows, left, prod, wins):
    f32, b16 = jnp.float32, jnp.bfloat16
    unpack(in_ref, rows)

    def piece(block, c):
        return rows[pl.ds(4 * block + c, DEV, PITCH), :]

    a, b = iota((128, 1024), 0), iota((128, 1024), 1)
    tile = ((a // 16 == b // 128) & (a % 16 == (b % 128) // 8)).astype(f32).astype(b16)
    halves = []
    keep = iota((512, 1024), 0) % 8 == iota((512, 1024), 1) % 8
    fold = (iota((64, 512), 0) == iota((64, 512), 1) // 8).astype(f32).astype(b16)
    for half in range(2):
        arrived = jnp.concatenate([piece(half, c) for c in range(ROWS)], axis=0).astype(b16)
        spread = dot_nn(arrived, tile)
        spread = jnp.where(keep, spread, 0.0).astype(b16)
        halves.append(dot_nn(fold, spread))
    for f in range(2):
        for s in range(NS):
            part = halves[s // 8][:, (s % 8) * 128 : (s % 8 + 1) * 128]
            re = part[(2 * f) * NS : (2 * f + 1) * NS]
            im = part[(2 * f + 1) * NS : (2 * f + 2) * NS]
            left[s * NS : (s + 1) * NS, 0:128] = re.astype(b16)
            left[s * NS : (s + 1) * NS, 128:256] = (-im).astype(b16)
            left[256 + s * NS : 256 + (s + 1) * NS, 0:128] = im.astype(b16)
            left[256 + s * NS : 256 + (s + 1) * NS, 128:256] = re.astype(b16)
        for n, blocks in ((0, 2), (2, 2), (4, 1)):
            right = jnp.concatenate(
                [
                    jnp.concatenate([piece(2 + n + m, 2 * f + part) for m in range(blocks)], axis=1)
                    for part in range(2)
                ],
                axis=0,
            ).astype(b16)
            prod[f * 512 : (f + 1) * 512, 128 * n : 128 * (n + blocks)] = dot_nn(left[...], right)
    first = rows[pl.ds(24, NS, PITCH * NPT), :][:, 64:80]
    lane = iota((NS, 128), 1)
    low = lane < 64
    for pair in range(NS // 2):
        begin = [
            jnp.broadcast_to(first[:, 2 * pair + e : 2 * pair + e + 1], (NS, 128)).astype(jnp.int32) for e in range(2)
        ]
        at = [lane + begin[0], lane + begin[1] + 64]
        index = [x & 127 for x in at]
        other = [(x + 64) & 127 for x in at]
        here = [lane + begin[0] + 64 < 128, lane + begin[1] < 128]
        for c in range(ROWS):
            base = c * 256 + 2 * pair * NS
            ahead = [None, None]
            for v in range(4, -1, -1):
                even, odd = [], []
                for e in range(2):
                    src = prod[base + e * NS : base + (e + 1) * NS, 128 * v : 128 * (v + 1)]
                    turned = jnp.take_along_axis(src, other[e], axis=1)
                    if v < 4:
                        even.append(jnp.take_along_axis(src, index[e], axis=1))
                        odd.append(jnp.where(here[e], turned, ahead[e]))
                    ahead[e] = turned
                if v < 4:
                    slot = c * 8 + pair
                    wins[pl.ds(2 * v * NS * PITCH + slot, NS, PITCH), :] = jnp.where(low, even[0], even[1])
                    wins[pl.ds((2 * v + 1) * NS * PITCH + slot, NS, PITCH), :] = jnp.where(low, odd[0], odd[1])
    for d in range(DEV):
        at = (d % NPT * NS + d // NPT) * PITCH
        out_ref[d] = wins[at : at + 32].astype(b16)


def inverse_kernel(in_ref, table_ref, out_any, rows, result, sems):
    unpack(in_ref, rows)
    pairs = NS // 2 // BLOCKS
    copies = []
    for block in range(BLOCKS):
        left = jnp.concatenate(
            [
                jnp.concatenate([rows[pl.ds(c * 8 + pair, DEV, PITCH), :].T for c in range(ROWS)], axis=1)
                for pair in range(block * pairs, (block + 1) * pairs)
            ],
            axis=0,
        ).astype(jnp.bfloat16)
        shots = pl.ds(2 * pairs * block, 2 * pairs)
        result[shots] = dot_nn(left, table_ref[...]).reshape(2 * pairs, SHARE, NT)
        copies.append(pltpu.make_async_copy(result.at[shots], out_any.at[shots], sems.at[block]))
        copies[-1].start()
    for copy in copies:
        copy.wait()


PARAMS = pltpu.CompilerParams(vmem_limit_bytes=VMEM)


def run_forward(shot_data, point_store, point_slot, taper_mask, recv_start):
    return pl.pallas_call(
        forward_kernel,
        out_shape=pltpu.VMEM((DEV, 32, 128), jnp.bfloat16), out_specs=pl.BlockSpec(memory_space=pltpu.VMEM),
        in_specs=[pl.BlockSpec(memory_space=m) for m in (pl.ANY, pl.ANY, pltpu.VMEM, pltpu.VMEM, pltpu.VMEM, pl.ANY)],
        scratch_shapes=[
            pltpu.VMEM((NS, NS, NT), jnp.bfloat16),
            pltpu.VMEM((GRID, NT), jnp.bfloat16),
            pltpu.VMEM((ROWS * DEV, NT), jnp.bfloat16),
            pltpu.VMEM((DEV * PITCH, 128), jnp.float32),
            pltpu.SemaphoreType.DMA((3,)),
        ],
        compiler_params=PARAMS,
        name="forward",
    )(shot_data, point_store, point_slot.reshape(1, NS), taper_mask, recv_start.reshape(1, NS), band_tables()[0])


def run_product(got):
    return pl.pallas_call(
        product_kernel,
        out_shape=pltpu.VMEM((DEV, 32, 128), jnp.bfloat16), out_specs=pl.BlockSpec(memory_space=pltpu.VMEM),
        scratch_shapes=[
            pltpu.VMEM((DEV * PITCH, 128), jnp.float32),
            pltpu.VMEM((512, 256), jnp.bfloat16),
            pltpu.VMEM((1024, 640), jnp.float32),
            pltpu.VMEM((DEV * PITCH, 128), jnp.float32),
        ],
        compiler_params=PARAMS,
        name="product",
        in_specs=[pl.BlockSpec(memory_space=pltpu.VMEM)],
    )(pltpu.with_memory_space_constraint(got, pltpu.VMEM))


def run_inverse(back):
    vmem = lambda x: pltpu.with_memory_space_constraint(x, pltpu.VMEM)
    return pl.pallas_call(
        inverse_kernel,
        in_specs=[pl.BlockSpec(memory_space=pltpu.VMEM)] * 2,
        out_specs=pl.BlockSpec(memory_space=pl.ANY),
        out_shape=jax.ShapeDtypeStruct((NS, SHARE, NT), jnp.float32),
        scratch_shapes=[
            pltpu.VMEM((DEV * PITCH, 128), jnp.float32),
            pltpu.VMEM((NS, SHARE, NT), jnp.float32),
            pltpu.SemaphoreType.DMA((BLOCKS,)),
        ],
        compiler_params=PARAMS,
        name="inverse",
    )(vmem(back), vmem(band_tables()[1]))


def per_device(shot_data, point_store, point_slot, taper_mask, recv_start):
    sent = run_forward(shot_data, point_store, point_slot, taper_mask, recv_start)
    got = lax.all_to_all(sent, ("shot", "pt"), 0, 0, tiled=True)
    back = lax.all_to_all(run_product(got), ("shot", "pt"), 0, 0, tiled=True)
    return run_inverse(back)


def solution(mesh):
    placed = (
        P("shot", "pt", None),
        P(("shot", "pt"), None, None),
        P("pt"),
        P("shot", "pt"),
        P("shot"),
    )
    return jax.shard_map(
        per_device, mesh=mesh, in_specs=placed, out_specs=P("shot", "pt", None), check_vma=False
    )
```

```python
import functools
import math

import jax
import jax.numpy as jnp
import numpy as np
from jax import lax
from jax.experimental import pallas as pl
from jax.experimental.pallas import tpu as pltpu
from jax.sharding import PartitionSpec as P


NT = 1024
NF = 256
GRID = 576
SPREAD = 512
DEV = 128
ROWS = 4
NS = 16
NPT = 8
SHARE = 64
VMEM = 56 * 1024 * 1024
BLOCKS = 8
PITCH = 40


def band_tables():
    phase = (np.arange(NT)[:, None] * np.arange(NF)[None, :]) % NT
    angle = phase.astype(np.float32) * np.float32(2.0 * math.pi / NT)
    cosine = np.cos(angle).T
    sine = np.sin(angle).T
    weights = np.where(np.arange(NF) == 0, 1.0, 2.0).astype(np.float32)[:, None] / np.float32(NT)
    forward = np.stack([cosine[0::2], -sine[0::2], cosine[1::2], -sine[1::2]])
    wc, ws = weights * cosine, -weights * sine
    inverse = np.stack([wc[0::2], ws[0::2], wc[1::2], ws[1::2]])
    forward = jnp.asarray(forward.reshape(ROWS * DEV, NT), jnp.bfloat16)
    inverse = jnp.asarray(inverse.reshape(ROWS * DEV, NT), jnp.bfloat16)
    return forward, inverse


def iota(shape, dim):
    return lax.broadcasted_iota(jnp.int32, shape, dim)


def dot_nt(left, right):
    return lax.dot_general(left, right, (((1,), (1,)), ((), ())), preferred_element_type=jnp.float32)


def dot_nn(left, right):
    return jnp.dot(left, right, preferred_element_type=jnp.float32)


def unpack(in_ref, rows):
    for d in range(DEV):
        rows[d * PITCH : d * PITCH + 32] = in_ref[d].astype(jnp.float32)


def order_matrix(slot_ref, mask_ref):
    f32, b16 = jnp.float32, jnp.bfloat16
    wide = NS * NS
    spread = (iota((NS, wide), 1) % NS == iota((NS, wide), 0)).astype(f32).astype(b16)
    owner = lax.shift_right_logical(slot_ref[...], 3).astype(f32).astype(b16)
    owner = dot_nn(jnp.broadcast_to(owner, (NS, NS)), spread)[0:1].astype(jnp.int32)
    taper = dot_nn(mask_ref[...].astype(f32).astype(b16), spread)
    taper = jnp.where(iota((NS, wide), 1) // NS == iota((NS, wide), 0), taper, 0.0)
    taper = jnp.sum(taper, axis=0, keepdims=True)
    r, l = iota((wide, wide), 0), iota((wide, wide), 1)
    return jnp.where((r // NS == l // NS) & (owner == r % NS), taper, 0.0).astype(b16)


def forward_kernel(
    shot_any, store_any, slot_any, mask_any, start_any, table_any, out_ref,
    shot, store, slot, mask, first, table, rows, sems,
):
    f32, b16 = jnp.float32, jnp.bfloat16
    parts = [pl.ds(0, 256), pl.ds(256, 256), pl.ds(512, 64)]
    pairs = [(slot_any, slot), (mask_any, mask), (start_any, first), (table_any, table), (shot_any, shot)]
    pairs += [(store_any.at[0, part], store.at[part]) for part in parts]
    loads = [pltpu.make_async_copy(src, dst, sems.at[n]) for n, (src, dst) in enumerate(pairs)]
    for load in loads:
        load.start()
    for load in loads[:3]:
        load.wait()
    order = order_matrix(slot, mask)
    pick = (iota((NS, 128), 1) - 64 == iota((NS, 128), 0)).astype(f32).astype(b16)
    start = first[...].astype(f32).astype(b16)
    start = dot_nn(jnp.broadcast_to(start, (NS, NS)), pick)[0:1]
    for c in range(ROWS):
        rows[pl.ds(28 + c, DEV, PITCH), :] = jnp.zeros((DEV, 128), f32)

    def put(block, value):
        for n in range(value.shape[1] // 128):
            for c in range(ROWS):
                rows[pl.ds(4 * (block + n) + c, DEV, PITCH), :] = value[c * DEV : (c + 1) * DEV, 128 * n : 128 * (n + 1)]

    loads[3].wait()
    loads[4].wait()
    spectra = dot_nt(table[...], shot[...].reshape(NS * NS, NT)).astype(b16)
    put(0, dot_nt(spectra, order))
    for h in range(2):
        loads[5 + h].wait()
        put(2 + 2 * h, dot_nt(table[...], store[256 * h : 256 * (h + 1)]))
    loads[7].wait()
    tail = jnp.concatenate([store[SPREAD:GRID], jnp.zeros((64, NT), b16)], axis=0)
    put(6, dot_nt(table[...], tail) + start)
    for d in range(DEV):
        out_ref[d] = rows[d * PITCH : d * PITCH + 32].astype(b16)


def product_kernel(in_ref, out_ref, rows, left, prod, wins):
    f32, b16 = jnp.float32, jnp.bfloat16
    unpack(in_ref, rows)

    def piece(block, c):
        return rows[pl.ds(4 * block + c, DEV, PITCH), :]

    a, b = iota((128, 1024), 0), iota((128, 1024), 1)
    tile = ((a // 16 == b // 128) & (a % 16 == (b % 128) // 8)).astype(f32).astype(b16)
    halves = []
    keep = iota((512, 1024), 0) % 8 == iota((512, 1024), 1) % 8
    fold = (iota((64, 512), 0) == iota((64, 512), 1) // 8).astype(f32).astype(b16)
    for half in range(2):
        arrived = jnp.concatenate([piece(half, c) for c in range(ROWS)], axis=0).astype(b16)
        spread = dot_nn(arrived, tile)
        spread = jnp.where(keep, spread, 0.0).astype(b16)
        halves.append(dot_nn(fold, spread))

    def product(f):
        for s in range(NS):
            part = halves[s // 8][:, (s % 8) * 128 : (s % 8 + 1) * 128]
            re = part[(2 * f) * NS : (2 * f + 1) * NS]
            im = part[(2 * f + 1) * NS : (2 * f + 2) * NS]
            left[f, s * NS : (s + 1) * NS, 0:128] = re.astype(b16)
            left[f, s * NS : (s + 1) * NS, 128:256] = (-im).astype(b16)
            left[f, 256 + s * NS : 256 + (s + 1) * NS, 0:128] = im.astype(b16)
            left[f, 256 + s * NS : 256 + (s + 1) * NS, 128:256] = re.astype(b16)
        for n, blocks in ((0, 2), (2, 2), (4, 1)):
            right = jnp.concatenate(
                [
                    jnp.concatenate([piece(2 + n + m, 2 * f + part) for m in range(blocks)], axis=1)
                    for part in range(2)
                ],
                axis=0,
            ).astype(b16)
            prod[f * 512 : (f + 1) * 512, 128 * n : 128 * (n + blocks)] = dot_nn(left[f], right)

    first = rows[pl.ds(24, NS, PITCH * NPT), :][:, 64:80]
    lane = iota((NS, 128), 1)
    low = lane < 64

    def cut(f, pair):
        begin = [
            jnp.broadcast_to(first[:, 2 * pair + e : 2 * pair + e + 1], (NS, 128)).astype(jnp.int32) for e in range(2)
        ]
        at = [lane + begin[0], lane + begin[1] + 64]
        index = [x & 127 for x in at]
        here = [at[0] < 128, (lane >= 64) | (at[1] < 128)]
        for c in (2 * f, 2 * f + 1):
            base = c * 256 + 2 * pair * NS
            ahead = [None, None]
            for v in range(4, -1, -1):
                tiles = []
                for e in range(2):
                    src = prod[base + e * NS : base + (e + 1) * NS, 128 * v : 128 * (v + 1)]
                    turned = jnp.take_along_axis(src, index[e], axis=1)
                    if v < 4:
                        tiles.append(jnp.where(here[e], turned, ahead[e]))
                    ahead[e] = turned
                if v < 4:
                    slot = c * 8 + pair
                    wins[pl.ds(2 * v * NS * PITCH + slot, NS, PITCH), :] = jnp.where(low, tiles[0], tiles[1])
                    wins[pl.ds((2 * v + 1) * NS * PITCH + slot, NS, PITCH), :] = jnp.where(low, tiles[1], tiles[0])

    product(0)
    for pair in range(4):
        cut(0, pair)
    product(1)
    for pair in range(4, 8):
        cut(0, pair)
    for pair in range(8):
        cut(1, pair)
    for d in range(DEV):
        at = (d % NPT * NS + d // NPT) * PITCH
        out_ref[d] = wins[at : at + 32].astype(b16)


def inverse_kernel(in_ref, table_ref, out_any, rows, result, sems):
    swap = lax.axis_index("pt") % 2
    unpack(in_ref, rows)
    pairs = NS // 2 // BLOCKS
    copies = []
    for block in range(BLOCKS):
        left = jnp.concatenate(
            [
                jnp.concatenate([rows[pl.ds(c * 8 + pair, DEV, PITCH), :].T for c in range(ROWS)], axis=1)
                for pair in range(block * pairs, (block + 1) * pairs)
            ],
            axis=0,
        ).astype(jnp.bfloat16)
        shots = pl.ds(2 * pairs * block, 2 * pairs)
        traces = dot_nn(left, table_ref[...])
        for pair in range(pairs):
            for e in range(2):
                place = 2 * (block * pairs + pair) + (swap if e == 0 else 1 - swap)
                result[place] = traces[(2 * pair + e) * SHARE : (2 * pair + e + 1) * SHARE]
        copies.append(pltpu.make_async_copy(result.at[shots], out_any.at[shots], sems.at[block]))
        copies[-1].start()
    for copy in copies:
        copy.wait()


PARAMS = pltpu.CompilerParams(vmem_limit_bytes=VMEM)


def run_forward(shot_data, point_store, point_slot, taper_mask, recv_start):
    return pl.pallas_call(
        forward_kernel,
        out_shape=pltpu.VMEM((DEV, 32, 128), jnp.bfloat16), out_specs=pl.BlockSpec(memory_space=pltpu.VMEM),
        in_specs=[pl.BlockSpec(memory_space=pl.ANY)] * 6,
        scratch_shapes=[
            pltpu.VMEM((NS, NS, NT), jnp.bfloat16),
            pltpu.VMEM((GRID, NT), jnp.bfloat16),
            pltpu.VMEM((1, NS), jnp.int32),
            pltpu.VMEM((NS, NS), jnp.int32),
            pltpu.VMEM((1, NS), jnp.int32),
            pltpu.VMEM((ROWS * DEV, NT), jnp.bfloat16),
            pltpu.VMEM((DEV * PITCH, 128), jnp.float32),
            pltpu.SemaphoreType.DMA((8,)),
        ],
        compiler_params=PARAMS,
        name="forward",
    )(shot_data, point_store, point_slot.reshape(1, NS), taper_mask, recv_start.reshape(1, NS), band_tables()[0])


def run_product(got):
    return pl.pallas_call(
        product_kernel,
        out_shape=pltpu.VMEM((DEV, 32, 128), jnp.bfloat16), out_specs=pl.BlockSpec(memory_space=pltpu.VMEM),
        scratch_shapes=[
            pltpu.VMEM((DEV * PITCH, 128), jnp.float32),
            pltpu.VMEM((2, 512, 256), jnp.bfloat16),
            pltpu.VMEM((1024, 640), jnp.float32),
            pltpu.VMEM((DEV * PITCH, 128), jnp.float32),
        ],
        compiler_params=PARAMS,
        name="product",
        in_specs=[pl.BlockSpec(memory_space=pltpu.VMEM)],
    )(pltpu.with_memory_space_constraint(got, pltpu.VMEM))


def run_inverse(back):
    vmem = lambda x: pltpu.with_memory_space_constraint(x, pltpu.VMEM)
    return pl.pallas_call(
        inverse_kernel,
        in_specs=[pl.BlockSpec(memory_space=pltpu.VMEM)] * 2,
        out_specs=pl.BlockSpec(memory_space=pl.ANY),
        out_shape=jax.ShapeDtypeStruct((NS, SHARE, NT), jnp.float32),
        scratch_shapes=[
            pltpu.VMEM((DEV * PITCH, 128), jnp.float32),
            pltpu.VMEM((NS, SHARE, NT), jnp.float32),
            pltpu.SemaphoreType.DMA((BLOCKS,)),
        ],
        compiler_params=PARAMS,
        name="inverse",
    )(vmem(back), vmem(band_tables()[1]))


def per_device(shot_data, point_store, point_slot, taper_mask, recv_start):
    sent = run_forward(shot_data, point_store, point_slot, taper_mask, recv_start)
    got = lax.all_to_all(sent, ("shot", "pt"), 0, 0, tiled=True)
    back = lax.all_to_all(run_product(got), ("shot", "pt"), 0, 0, tiled=True)
    return run_inverse(back)


def solution(mesh):
    placed = (
        P("shot", "pt", None),
        P(("shot", "pt"), None, None),
        P("pt"),
        P("shot", "pt"),
        P("shot"),
    )
    return jax.shard_map(
        per_device, mesh=mesh, in_specs=placed, out_specs=P("shot", "pt", None), check_vma=False
    )
```

```python
import functools
import math

import jax
import jax.numpy as jnp
import numpy as np
from jax import lax
from jax.experimental import pallas as pl
from jax.experimental.pallas import tpu as pltpu
from jax.sharding import PartitionSpec as P


NT = 1024
NF = 256
GRID = 576
SPREAD = 512
DEV = 128
ROWS = 4
NS = 16
NPT = 8
SHARE = 64
VMEM = 56 * 1024 * 1024
BLOCKS = 8
PITCH = 40


def band_tables():
    phase = (np.arange(NT)[:, None] * np.arange(NF)[None, :]) % NT
    angle = phase.astype(np.float32) * np.float32(2.0 * math.pi / NT)
    cosine = np.cos(angle).T
    sine = np.sin(angle).T
    weights = np.where(np.arange(NF) == 0, 1.0, 2.0).astype(np.float32)[:, None] / np.float32(NT)
    forward = np.stack([cosine, -sine], axis=1)
    wc, ws = weights * cosine, -weights * sine
    inverse = np.stack([wc[0::2], ws[0::2], wc[1::2], ws[1::2]])
    forward = jnp.asarray(forward.reshape(ROWS * DEV, NT), jnp.bfloat16)
    inverse = jnp.asarray(inverse.reshape(ROWS * DEV, NT), jnp.bfloat16)
    return forward, inverse


def iota(shape, dim):
    return lax.broadcasted_iota(jnp.int32, shape, dim)


def dot_nt(left, right):
    return lax.dot_general(left, right, (((1,), (1,)), ((), ())), preferred_element_type=jnp.float32)


def dot_nn(left, right):
    return jnp.dot(left, right, preferred_element_type=jnp.float32)


def unpack(in_ref, rows):
    for d in range(DEV):
        rows[d * PITCH : d * PITCH + 32] = in_ref[d].astype(jnp.float32)


def order_matrix(slot_ref, mask_ref):
    f32, b16 = jnp.float32, jnp.bfloat16
    wide = NS * NS
    spread = (iota((NS, wide), 1) % NS == iota((NS, wide), 0)).astype(f32).astype(b16)
    owner = lax.shift_right_logical(slot_ref[...], 3).astype(f32).astype(b16)
    owner = dot_nn(jnp.broadcast_to(owner, (NS, NS)), spread)[0:1].astype(jnp.int32)
    taper = dot_nn(mask_ref[...].astype(f32).astype(b16), spread)
    taper = jnp.where(iota((NS, wide), 1) // NS == iota((NS, wide), 0), taper, 0.0)
    taper = jnp.sum(taper, axis=0, keepdims=True)
    r, l = iota((wide, wide), 0), iota((wide, wide), 1)
    return jnp.where((r // NS == l // NS) & (owner == r % NS), taper, 0.0).astype(b16)


def forward_kernel(
    shot_any, store_any, slot_any, mask_any, start_any, table_any, out_ref,
    shot, store, slot, mask, first, table, sems,
):
    f32, b16 = jnp.float32, jnp.bfloat16
    parts = [pl.ds(0, 256), pl.ds(256, 256), pl.ds(512, 64)]
    pairs = [(slot_any, slot), (mask_any, mask), (start_any, first), (table_any, table), (shot_any, shot)]
    pairs += [(store_any.at[0, part], store.at[part]) for part in parts]
    loads = [pltpu.make_async_copy(src, dst, sems.at[n]) for n, (src, dst) in enumerate(pairs)]
    for load in loads:
        load.start()
    for load in loads[:3]:
        load.wait()
    order = order_matrix(slot, mask)
    pick = (iota((NS, 128), 1) - 64 == iota((NS, 128), 0)).astype(f32).astype(b16)
    start = first[...].astype(f32).astype(b16)
    start = dot_nn(jnp.broadcast_to(start, (NS, NS)), pick)[0:1]
    def put(block, value):
        for n in range(value.shape[1] // 128):
            out_ref[:, block + n] = value[:, 128 * n : 128 * (n + 1)].reshape(DEV, ROWS, 128).astype(b16)

    loads[3].wait()
    loads[4].wait()
    spectra = dot_nt(table[...], shot[...].reshape(NS * NS, NT)).astype(b16)
    put(0, dot_nt(spectra, order))
    for h in range(2):
        loads[5 + h].wait()
        put(2 + 2 * h, dot_nt(table[...], store[256 * h : 256 * (h + 1)]))
    loads[7].wait()
    tail = jnp.concatenate([store[SPREAD:GRID], jnp.zeros((64, NT), b16)], axis=0)
    put(6, dot_nt(table[...], tail) + start)


def product_kernel(in_ref, out_ref, rows, left, prod, wins):
    f32, b16 = jnp.float32, jnp.bfloat16
    for block in range(7):
        rows[block] = in_ref[:, block].astype(f32).reshape(DEV * ROWS, 128)

    def piece(block, c):
        return rows[block, pl.ds(c, DEV, ROWS), :]

    a, b = iota((128, 1024), 0), iota((128, 1024), 1)
    tile = ((a // 16 == b // 128) & (a % 16 == (b % 128) // 8)).astype(f32).astype(b16)
    halves = []
    keep = iota((512, 1024), 0) % 8 == iota((512, 1024), 1) % 8
    fold = (iota((64, 512), 0) == iota((64, 512), 1) // 8).astype(f32).astype(b16)
    for half in range(2):
        arrived = jnp.concatenate([piece(half, c) for c in range(ROWS)], axis=0).astype(b16)
        spread = dot_nn(arrived, tile)
        spread = jnp.where(keep, spread, 0.0).astype(b16)
        halves.append(dot_nn(fold, spread))

    def product(f):
        for s in range(NS):
            part = halves[s // 8][:, (s % 8) * 128 : (s % 8 + 1) * 128]
            re = part[(2 * f) * NS : (2 * f + 1) * NS]
            im = part[(2 * f + 1) * NS : (2 * f + 2) * NS]
            left[f, s * NS : (s + 1) * NS, 0:128] = re.astype(b16)
            left[f, s * NS : (s + 1) * NS, 128:256] = (-im).astype(b16)
            left[f, 256 + s * NS : 256 + (s + 1) * NS, 0:128] = im.astype(b16)
            left[f, 256 + s * NS : 256 + (s + 1) * NS, 128:256] = re.astype(b16)
        for n, blocks in ((0, 2), (2, 2), (4, 1)):
            right = jnp.concatenate(
                [
                    jnp.concatenate([piece(2 + n + m, 2 * f + part) for m in range(blocks)], axis=1)
                    for part in range(2)
                ],
                axis=0,
            ).astype(b16)
            prod[f * 512 : (f + 1) * 512, 128 * n : 128 * (n + blocks)] = dot_nn(left[f], right)

    first = rows[6, pl.ds(0, NS, ROWS * NPT), :][:, 64:80]
    lane = iota((NS, 128), 1)
    low = lane < 64

    def cut(f, pair):
        begin = [
            jnp.broadcast_to(first[:, 2 * pair + e : 2 * pair + e + 1], (NS, 128)).astype(jnp.int32) for e in range(2)
        ]
        at = [lane + begin[0], lane + begin[1] + 64]
        index = [x & 127 for x in at]
        here = [at[0] < 128, (lane >= 64) | (at[1] < 128)]
        for c in (2 * f, 2 * f + 1):
            base = c * 256 + 2 * pair * NS
            ahead = [None, None]
            for v in range(4, -1, -1):
                tiles = []
                for e in range(2):
                    src = prod[base + e * NS : base + (e + 1) * NS, 128 * v : 128 * (v + 1)]
                    turned = jnp.take_along_axis(src, index[e], axis=1)
                    if v < 4:
                        tiles.append(jnp.where(here[e], turned, ahead[e]))
                    ahead[e] = turned
                if v < 4:
                    slot = c * 8 + pair
                    wins[pl.ds(2 * v * NS * PITCH + slot, NS, PITCH), :] = jnp.where(low, tiles[0], tiles[1])
                    wins[pl.ds((2 * v + 1) * NS * PITCH + slot, NS, PITCH), :] = jnp.where(low, tiles[1], tiles[0])

    product(0)
    for pair in range(4):
        cut(0, pair)
    product(1)
    for pair in range(4, 8):
        cut(0, pair)
    for pair in range(8):
        cut(1, pair)
    for d in range(DEV):
        at = (d % NPT * NS + d // NPT) * PITCH
        out_ref[d] = wins[at : at + 32].astype(b16)


def inverse_kernel(in_ref, table_ref, out_any, rows, result, sems):
    swap = lax.axis_index("pt") % 2
    unpack(in_ref, rows)
    pairs = NS // 2 // BLOCKS
    copies = []
    for block in range(BLOCKS):
        left = jnp.concatenate(
            [
                jnp.concatenate([rows[pl.ds(c * 8 + pair, DEV, PITCH), :].T for c in range(ROWS)], axis=1)
                for pair in range(block * pairs, (block + 1) * pairs)
            ],
            axis=0,
        ).astype(jnp.bfloat16)
        shots = pl.ds(2 * pairs * block, 2 * pairs)
        traces = dot_nn(left, table_ref[...])
        for pair in range(pairs):
            for e in range(2):
                place = 2 * (block * pairs + pair) + (swap if e == 0 else 1 - swap)
                result[place] = traces[(2 * pair + e) * SHARE : (2 * pair + e + 1) * SHARE]
        copies.append(pltpu.make_async_copy(result.at[shots], out_any.at[shots], sems.at[block]))
        copies[-1].start()
    for copy in copies:
        copy.wait()


PARAMS = pltpu.CompilerParams(vmem_limit_bytes=VMEM)


def run_forward(shot_data, point_store, point_slot, taper_mask, recv_start):
    return pl.pallas_call(
        forward_kernel,
        out_shape=pltpu.VMEM((DEV, 7, ROWS, 128), jnp.bfloat16), out_specs=pl.BlockSpec(memory_space=pltpu.VMEM),
        in_specs=[pl.BlockSpec(memory_space=pl.ANY)] * 6,
        scratch_shapes=[
            pltpu.VMEM((NS, NS, NT), jnp.bfloat16),
            pltpu.VMEM((GRID, NT), jnp.bfloat16),
            pltpu.VMEM((1, NS), jnp.int32),
            pltpu.VMEM((NS, NS), jnp.int32),
            pltpu.VMEM((1, NS), jnp.int32),
            pltpu.VMEM((ROWS * DEV, NT), jnp.bfloat16),
            pltpu.SemaphoreType.DMA((8,)),
        ],
        compiler_params=PARAMS,
        name="forward",
    )(shot_data, point_store, point_slot.reshape(1, NS), taper_mask, recv_start.reshape(1, NS), band_tables()[0])


def run_product(got):
    return pl.pallas_call(
        product_kernel,
        out_shape=pltpu.VMEM((DEV, 32, 128), jnp.bfloat16), out_specs=pl.BlockSpec(memory_space=pltpu.VMEM),
        scratch_shapes=[
            pltpu.VMEM((7, DEV * ROWS, 128), jnp.float32),
            pltpu.VMEM((2, 512, 256), jnp.bfloat16),
            pltpu.VMEM((1024, 640), jnp.float32),
            pltpu.VMEM((DEV * PITCH, 128), jnp.float32),
        ],
        compiler_params=PARAMS,
        name="product",
        in_specs=[pl.BlockSpec(memory_space=pltpu.VMEM)],
    )(pltpu.with_memory_space_constraint(got, pltpu.VMEM))


def run_inverse(back):
    vmem = lambda x: pltpu.with_memory_space_constraint(x, pltpu.VMEM)
    return pl.pallas_call(
        inverse_kernel,
        in_specs=[pl.BlockSpec(memory_space=pltpu.VMEM)] * 2,
        out_specs=pl.BlockSpec(memory_space=pl.ANY),
        out_shape=jax.ShapeDtypeStruct((NS, SHARE, NT), jnp.float32),
        scratch_shapes=[
            pltpu.VMEM((DEV * PITCH, 128), jnp.float32),
            pltpu.VMEM((NS, SHARE, NT), jnp.float32),
            pltpu.SemaphoreType.DMA((BLOCKS,)),
        ],
        compiler_params=PARAMS,
        name="inverse",
    )(vmem(back), vmem(band_tables()[1]))


def per_device(shot_data, point_store, point_slot, taper_mask, recv_start):
    sent = run_forward(shot_data, point_store, point_slot, taper_mask, recv_start)
    got = lax.all_to_all(sent, ("shot", "pt"), 0, 0, tiled=True)
    back = lax.all_to_all(run_product(got), ("shot", "pt"), 0, 0, tiled=True)
    return run_inverse(back)


def solution(mesh):
    placed = (
        P("shot", "pt", None),
        P(("shot", "pt"), None, None),
        P("pt"),
        P("shot", "pt"),
        P("shot"),
    )
    return jax.shard_map(
        per_device, mesh=mesh, in_specs=placed, out_specs=P("shot", "pt", None), check_vma=False
    )
```

```python
import functools
import math

import jax
import jax.numpy as jnp
import numpy as np
from jax import lax
from jax.experimental import pallas as pl
from jax.experimental.pallas import tpu as pltpu
from jax.sharding import PartitionSpec as P


NT = 1024
NF = 256
GRID = 576
SPREAD = 512
DEV = 128
ROWS = 4
NS = 16
NPT = 8
SHARE = 64
VMEM = 56 * 1024 * 1024
PITCH = 40


def band_tables():
    phase = (np.arange(NT)[:, None] * np.arange(NF)[None, :]) % NT
    angle = phase.astype(np.float32) * np.float32(2.0 * math.pi / NT)
    cosine = np.cos(angle).T
    sine = np.sin(angle).T
    weights = np.where(np.arange(NF) == 0, 1.0, 2.0).astype(np.float32)[:, None] / np.float32(NT)
    forward = np.stack([cosine, -sine], axis=1)
    inverse = np.stack([weights * cosine, -weights * sine], axis=1)
    forward = jnp.asarray(forward.reshape(ROWS * DEV, NT), jnp.bfloat16)
    inverse = jnp.asarray(inverse.reshape(ROWS * DEV, NT), jnp.bfloat16)
    return forward, inverse


def iota(shape, dim):
    return lax.broadcasted_iota(jnp.int32, shape, dim)


def dot_nt(left, right):
    return lax.dot_general(left, right, (((1,), (1,)), ((), ())), preferred_element_type=jnp.float32)


def dot_nn(left, right):
    return jnp.dot(left, right, preferred_element_type=jnp.float32)


def order_matrix(slot_ref, mask_ref):
    f32, b16 = jnp.float32, jnp.bfloat16
    wide = NS * NS
    spread = (iota((NS, wide), 1) % NS == iota((NS, wide), 0)).astype(f32).astype(b16)
    owner = lax.shift_right_logical(slot_ref[...], 3).astype(f32).astype(b16)
    owner = dot_nn(jnp.broadcast_to(owner, (NS, NS)), spread)[0:1].astype(jnp.int32)
    taper = dot_nn(mask_ref[...].astype(f32).astype(b16), spread)
    taper = jnp.where(iota((NS, wide), 1) // NS == iota((NS, wide), 0), taper, 0.0)
    taper = jnp.sum(taper, axis=0, keepdims=True)
    r, l = iota((wide, wide), 0), iota((wide, wide), 1)
    return jnp.where((r // NS == l // NS) & (owner == r % NS), taper, 0.0).astype(b16)


def forward_kernel(
    shot_any, store_any, slot_any, mask_any, start_any, table_any, out_ref,
    shot, store, slot, mask, first, table, sems,
):
    f32, b16 = jnp.float32, jnp.bfloat16
    pairs = [(slot_any, slot), (mask_any, mask), (start_any, first), (table_any, table), (shot_any, shot)]
    pairs += [(store_any.at[0], store.at[pl.ds(0, GRID)])]
    loads = [pltpu.make_async_copy(src, dst, sems.at[n]) for n, (src, dst) in enumerate(pairs)]
    for load in loads:
        load.start()
    store[GRID:] = jnp.zeros((64, NT), b16)
    for load in loads[:3]:
        load.wait()
    order = order_matrix(slot, mask)
    pick = (iota((NS, 128), 1) - 64 == iota((NS, 128), 0)).astype(f32).astype(b16)
    start = first[...].astype(f32).astype(b16)
    start = dot_nn(jnp.broadcast_to(start, (NS, NS)), pick)[0:1]
    def put(block, value):
        for n in range(value.shape[1] // 128):
            out_ref[:, block + n] = value[:, 128 * n : 128 * (n + 1)].reshape(DEV, ROWS, 128).astype(b16)

    for load in loads[3:]:
        load.wait()
    spectra = dot_nt(table[...], shot[...].reshape(NS * NS, NT)).astype(b16)
    gathers = dot_nt(table[...], store[...])
    put(2, gathers[:, 0:SPREAD])
    put(6, gathers[:, SPREAD:] + start)
    put(0, dot_nt(spectra, order))


def product_kernel(in_ref, out_ref, rows, left, prod, wins):
    f32, b16 = jnp.float32, jnp.bfloat16
    for block in range(7):
        rows[block] = in_ref[:, block].astype(f32).reshape(DEV * ROWS, 128)

    def piece(block, c):
        return rows[block, pl.ds(c, DEV, ROWS), :]

    a, b = iota((128, 1024), 0), iota((128, 1024), 1)
    tile = ((a // 16 == b // 128) & (a % 16 == (b % 128) // 8)).astype(f32).astype(b16)
    keep = iota((256, 1024), 0) % 8 == iota((256, 1024), 1) % 8
    fold = (iota((32, 256), 0) == iota((32, 256), 1) // 8).astype(f32).astype(b16)

    def product(f):
        for half in range(2):
            arrived = jnp.concatenate([piece(half, c) for c in (2 * f, 2 * f + 1)], axis=0).astype(b16)
            spread = jnp.where(keep, dot_nn(arrived, tile), 0.0).astype(b16)
            folded = dot_nn(fold, spread)
            for n in range(8):
                re, im = folded[0:NS, n * 128 : (n + 1) * 128], folded[NS:, n * 128 : (n + 1) * 128]
                top = (half * 8 + n) * NS
                left[f, top : top + NS, 0:128] = re.astype(b16)
                left[f, top : top + NS, 128:256] = (-im).astype(b16)
                left[f, 256 + top : 256 + top + NS, 0:128] = im.astype(b16)
                left[f, 256 + top : 256 + top + NS, 128:256] = re.astype(b16)
        for n, blocks in ((0, 2), (2, 2), (4, 1)):
            right = jnp.concatenate(
                [
                    jnp.concatenate([piece(2 + n + m, 2 * f + part) for m in range(blocks)], axis=1)
                    for part in range(2)
                ],
                axis=0,
            ).astype(b16)
            prod[f * 512 : (f + 1) * 512, 128 * n : 128 * (n + blocks)] = dot_nn(left[f], right)

    first = rows[6, pl.ds(0, NS, ROWS * NPT), :][:, 64:80]
    lane = iota((NS, 128), 1)
    low = lane < 64

    def cut(f, pair):
        begin = [
            jnp.broadcast_to(first[:, 2 * pair + e : 2 * pair + e + 1], (NS, 128)).astype(jnp.int32) for e in range(2)
        ]
        at = [lane + begin[0], lane + begin[1] + 64]
        index = [x & 127 for x in at]
        here = [at[0] < 128, (lane >= 64) | (at[1] < 128)]
        for c in (2 * f, 2 * f + 1):
            base = c * 256 + 2 * pair * NS
            ahead = [None, None]
            for v in range(4, -1, -1):
                tiles = []
                for e in range(2):
                    src = prod[base + e * NS : base + (e + 1) * NS, 128 * v : 128 * (v + 1)]
                    turned = jnp.take_along_axis(src, index[e], axis=1)
                    if v < 4:
                        tiles.append(jnp.where(here[e], turned, ahead[e]))
                    ahead[e] = turned
                if v < 4:
                    slot = pair * ROWS + c
                    wins[pl.ds(2 * v * NS * PITCH + slot, NS, PITCH), :] = jnp.where(low, tiles[0], tiles[1])
                    wins[pl.ds((2 * v + 1) * NS * PITCH + slot, NS, PITCH), :] = jnp.where(low, tiles[1], tiles[0])

    product(0)
    product(1)
    for pair in range(8):
        cut(0, pair)
    for pair in range(8):
        cut(1, pair)
    for d in range(DEV):
        at = (d % NPT * NS + d // NPT) * PITCH
        out_ref[d] = wins[at : at + 32].reshape(NS // 2, ROWS, 128).astype(b16)


def inverse_kernel(in_ref, table_ref, out_any, result, sems):
    swap = lax.axis_index("pt") % 2
    copies = []
    for pair in range(NS // 2):
        left = in_ref[:, pair].reshape(DEV * ROWS, 128).T
        traces = dot_nn(left, table_ref[...])
        for e in range(2):
            result[2 * pair + (swap if e == 0 else 1 - swap)] = traces[e * SHARE : (e + 1) * SHARE]
        shots = pl.ds(2 * pair, 2)
        copies.append(pltpu.make_async_copy(result.at[shots], out_any.at[shots], sems.at[pair]))
        copies[-1].start()
    for copy in copies:
        copy.wait()


PARAMS = pltpu.CompilerParams(vmem_limit_bytes=VMEM)


def run_forward(shot_data, point_store, point_slot, taper_mask, recv_start):
    return pl.pallas_call(
        forward_kernel,
        out_shape=pltpu.VMEM((DEV, 7, ROWS, 128), jnp.bfloat16), out_specs=pl.BlockSpec(memory_space=pltpu.VMEM),
        in_specs=[pl.BlockSpec(memory_space=pl.ANY)] * 6,
        scratch_shapes=[
            pltpu.VMEM((NS, NS, NT), jnp.bfloat16),
            pltpu.VMEM((GRID + 64, NT), jnp.bfloat16),
            pltpu.VMEM((1, NS), jnp.int32),
            pltpu.VMEM((NS, NS), jnp.int32),
            pltpu.VMEM((1, NS), jnp.int32),
            pltpu.VMEM((ROWS * DEV, NT), jnp.bfloat16),
            pltpu.SemaphoreType.DMA((6,)),
        ],
        compiler_params=PARAMS,
        name="forward",
    )(shot_data, point_store, point_slot.reshape(1, NS), taper_mask, recv_start.reshape(1, NS), band_tables()[0])


def run_product(got):
    return pl.pallas_call(
        product_kernel,
        out_shape=pltpu.VMEM((DEV, NS // 2, ROWS, 128), jnp.bfloat16), out_specs=pl.BlockSpec(memory_space=pltpu.VMEM),
        scratch_shapes=[
            pltpu.VMEM((7, DEV * ROWS, 128), jnp.float32),
            pltpu.VMEM((2, 512, 256), jnp.bfloat16),
            pltpu.VMEM((1024, 640), jnp.float32),
            pltpu.VMEM((DEV * PITCH, 128), jnp.float32),
        ],
        compiler_params=PARAMS,
        name="product",
        in_specs=[pl.BlockSpec(memory_space=pltpu.VMEM)],
    )(pltpu.with_memory_space_constraint(got, pltpu.VMEM))


def run_inverse(back):
    vmem = lambda x: pltpu.with_memory_space_constraint(x, pltpu.VMEM)
    return pl.pallas_call(
        inverse_kernel,
        in_specs=[pl.BlockSpec(memory_space=pltpu.VMEM)] * 2,
        out_specs=pl.BlockSpec(memory_space=pl.ANY),
        out_shape=jax.ShapeDtypeStruct((NS, SHARE, NT), jnp.float32),
        scratch_shapes=[
            pltpu.VMEM((NS, SHARE, NT), jnp.float32),
            pltpu.SemaphoreType.DMA((NS // 2,)),
        ],
        compiler_params=PARAMS,
        name="inverse",
    )(vmem(back), vmem(band_tables()[1]))


def per_device(shot_data, point_store, point_slot, taper_mask, recv_start):
    sent = run_forward(shot_data, point_store, point_slot, taper_mask, recv_start)
    got = lax.all_to_all(sent, ("shot", "pt"), 0, 0, tiled=True)
    back = lax.all_to_all(run_product(got), ("shot", "pt"), 0, 0, tiled=True)
    return run_inverse(back)


def solution(mesh):
    placed = (
        P("shot", "pt", None),
        P(("shot", "pt"), None, None),
        P("pt"),
        P("shot", "pt"),
        P("shot"),
    )
    return jax.shard_map(
        per_device, mesh=mesh, in_specs=placed, out_specs=P("shot", "pt", None), check_vma=False
    )
```

```python
import functools
import math

import jax
import jax.numpy as jnp
import numpy as np
from jax import lax
from jax.experimental import pallas as pl
from jax.experimental.pallas import tpu as pltpu
from jax.sharding import PartitionSpec as P


NT = 1024
NF = 256
GRID = 576
SPREAD = 512
DEV = 128
ROWS = 4
NS = 16
NPT = 8
SHARE = 64
SHOTROWS = NS * NS
VMEM = 56 * 1024 * 1024
PITCH = 40


def band_tables():
    phase = (np.arange(NT)[:, None] * np.arange(NF)[None, :]) % NT
    angle = phase.astype(np.float32) * np.float32(2.0 * math.pi / NT)
    cosine = np.cos(angle).T
    sine = np.sin(angle).T
    weights = np.where(np.arange(NF) == 0, 1.0, 2.0).astype(np.float32)[:, None] / np.float32(NT)
    forward = np.stack([cosine, -sine], axis=1)
    inverse = np.stack([weights * cosine, -weights * sine], axis=1)
    forward = jnp.asarray(forward.reshape(ROWS * DEV, NT).T, jnp.bfloat16)
    inverse = jnp.asarray(inverse.reshape(ROWS * DEV, NT), jnp.bfloat16)
    return forward, inverse


def iota(shape, dim):
    return lax.broadcasted_iota(jnp.int32, shape, dim)


def dot_nt(left, right):
    return lax.dot_general(left, right, (((1,), (1,)), ((), ())), preferred_element_type=jnp.float32)


def dot_nn(left, right):
    return jnp.dot(left, right, preferred_element_type=jnp.float32)


def order_matrix(slot_ref, mask_ref):
    f32, b16 = jnp.float32, jnp.bfloat16
    wide = NS * NS
    spread = (iota((NS, wide), 1) % NS == iota((NS, wide), 0)).astype(f32).astype(b16)
    owner = lax.shift_right_logical(slot_ref[...], 3).astype(f32).astype(b16)
    owner = dot_nn(jnp.broadcast_to(owner, (NS, NS)), spread)[0:1].astype(jnp.int32)
    taper = dot_nn(mask_ref[...].astype(f32).astype(b16), spread)
    taper = jnp.where(iota((NS, wide), 1) // NS == iota((NS, wide), 0), taper, 0.0)
    taper = jnp.sum(taper, axis=0, keepdims=True)
    r, l = iota((wide, wide), 0), iota((wide, wide), 1)
    return jnp.where((r // NS == l // NS) & (owner == r % NS), taper, 0.0).astype(b16)


def forward_kernel(
    shot_any, store_any, slot_any, mask_any, start_any, table_any, out_ref,
    shot, store, slot, mask, first, table, sems,
):
    f32, b16 = jnp.float32, jnp.bfloat16
    pairs = [(slot_any, slot), (mask_any, mask), (start_any, first), (table_any, table)]
    pairs += [(shot_any, shot), (store_any.at[0], store)]
    loads = [pltpu.make_async_copy(src, dst, sems.at[n]) for n, (src, dst) in enumerate(pairs)]
    for load in loads:
        load.start()
    for load in loads[:3]:
        load.wait()
    order = order_matrix(slot, mask)
    start = jnp.broadcast_to(first[...].astype(f32).astype(b16), (NS, NS))
    start = jnp.where(iota((NS, NS), 0) == iota((NS, NS), 1), start, 0).astype(b16)
    start = dot_nn(start, jnp.ones((NS, ROWS * DEV), b16)).astype(b16)
    start = jnp.concatenate([start, jnp.zeros((64 - NS, ROWS * DEV), b16)], axis=0)
    for load in loads[3:]:
        load.wait()

    def put(block, value):
        for n in range(value.shape[0] // 128):
            out_ref[:, block + n] = value[128 * n : 128 * (n + 1)].T.reshape(DEV, ROWS, 128)

    spectra = dot_nn(shot[...].reshape(SHOTROWS, NT), table[...]).astype(b16)
    put(2, jnp.concatenate([dot_nn(store[...], table[...]).astype(b16), start], axis=0))
    put(0, dot_nn(order, spectra).astype(b16))


def product_kernel(in_ref, out_ref, rows, left, prod, wins):
    f32, b16 = jnp.float32, jnp.bfloat16
    for block in range(7):
        for s in range(NS):
            part = in_ref[s * NPT : (s + 1) * NPT, block].astype(f32)
            rows[block, s * PITCH : s * PITCH + NPT * ROWS] = part.reshape(NPT * ROWS, 128)

    def piece(block, c, p):
        return rows[block, pl.ds(p * ROWS + c, NS, PITCH), :]

    arrived = jnp.concatenate(
        [piece(half, c, p) for p in range(NPT) for half in range(2) for c in range(ROWS)], axis=0
    ).astype(b16)
    place = (iota((NS, 128), 0) == iota((NS, 128), 1) % NS).astype(f32).astype(b16)
    zero = jnp.zeros((NS, 128), b16)
    own = (iota((8, 256), 1) % 128 // NS)[None]
    spectra = []
    for n in range(4):
        tile = [[place if s == 2 * n + m else zero for s in range(8)] for m in range(2)]
        tile = jnp.concatenate([jnp.concatenate(rows_of, axis=0) for rows_of in tile], axis=1)
        spread = dot_nn(arrived, tile).reshape(NPT, 16, 8, 256)
        chosen = spread[0]
        for p in range(1, NPT):
            chosen = jnp.where(own == p, spread[p], chosen)
        spectra.append(chosen.reshape(128, 256))

    def product(f):
        for s in range(NS):
            top = s // 8 * 64 + 2 * f * NS
            cols = slice(s % 2 * 128, (s % 2 + 1) * 128)
            part = spectra[s % 8 // 2]
            re, im = part[top : top + NS, cols], part[top + NS : top + 2 * NS, cols]
            left[f, s * NS : (s + 1) * NS, 0:128] = re.astype(b16)
            left[f, s * NS : (s + 1) * NS, 128:256] = (-im).astype(b16)
            left[f, 256 + s * NS : 256 + (s + 1) * NS, 0:128] = im.astype(b16)
            left[f, 256 + s * NS : 256 + (s + 1) * NS, 128:256] = re.astype(b16)
        for n, blocks in ((0, 2), (2, 2), (4, 1)):
            right = jnp.concatenate(
                [
                    jnp.concatenate([piece(2 + n + m, 2 * f + part, p) for m in range(blocks)], axis=1)
                    for part in range(2)
                    for p in range(NPT)
                ],
                axis=0,
            ).astype(b16)
            prod[f * 512 : (f + 1) * 512, 128 * n : 128 * (n + blocks)] = dot_nn(left[f], right)

    first = piece(6, 0, 0)[:, 64:80]
    lane = iota((NS, 128), 1)
    low = lane < 64

    def cut(f, pair):
        begin = [
            jnp.broadcast_to(first[:, 2 * pair + e : 2 * pair + e + 1], (NS, 128)).astype(jnp.int32) for e in range(2)
        ]
        at = [lane + begin[0], lane + begin[1] + 64]
        index = [x & 127 for x in at]
        here = [at[0] < 128, (lane >= 64) | (at[1] < 128)]
        for c in (2 * f, 2 * f + 1):
            base = c * 256 + 2 * pair * NS
            ahead = [None, None]
            for v in range(4, -1, -1):
                tiles = []
                for e in range(2):
                    src = prod[base + e * NS : base + (e + 1) * NS, 128 * v : 128 * (v + 1)]
                    turned = jnp.take_along_axis(src, index[e], axis=1)
                    if v < 4:
                        tiles.append(jnp.where(here[e], turned, ahead[e]))
                    ahead[e] = turned
                if v < 4:
                    slot = pair * ROWS + c
                    wins[pl.ds(2 * v * NS * PITCH + slot, NS, PITCH), :] = jnp.where(low, tiles[0], tiles[1])
                    wins[pl.ds((2 * v + 1) * NS * PITCH + slot, NS, PITCH), :] = jnp.where(low, tiles[1], tiles[0])

    product(0)
    product(1)
    for pair in range(8):
        cut(0, pair)
    for pair in range(8):
        cut(1, pair)
    for d in range(DEV):
        at = (d % NPT * NS + d // NPT) * PITCH
        out_ref[d] = wins[at : at + 32].reshape(NS // 2, ROWS, 128).astype(b16)


def inverse_kernel(in_ref, table_ref, out_any, result, sems):
    swap = lax.axis_index("pt") % 2
    copies = []
    for pair in range(NS // 2):
        left = in_ref[:, pair].reshape(DEV * ROWS, 128).T
        traces = dot_nn(left, table_ref[...])
        for e in range(2):
            result[2 * pair + (swap if e == 0 else 1 - swap)] = traces[e * SHARE : (e + 1) * SHARE]
        shots = pl.ds(2 * pair, 2)
        copies.append(pltpu.make_async_copy(result.at[shots], out_any.at[shots], sems.at[pair]))
        copies[-1].start()
    for copy in copies:
        copy.wait()


PARAMS = pltpu.CompilerParams(vmem_limit_bytes=VMEM)


def run_forward(shot_data, point_store, point_slot, taper_mask, recv_start):
    return pl.pallas_call(
        forward_kernel,
        out_shape=pltpu.VMEM((DEV, 7, ROWS, 128), jnp.bfloat16),
        out_specs=pl.BlockSpec(memory_space=pltpu.VMEM),
        in_specs=[pl.BlockSpec(memory_space=pl.ANY)] * 6,
        scratch_shapes=[
            pltpu.VMEM((NS, NS, NT), jnp.bfloat16),
            pltpu.VMEM((GRID, NT), jnp.bfloat16),
            pltpu.VMEM((1, NS), jnp.int32),
            pltpu.VMEM((NS, NS), jnp.int32),
            pltpu.VMEM((1, NS), jnp.int32),
            pltpu.VMEM((NT, ROWS * DEV), jnp.bfloat16),
            pltpu.SemaphoreType.DMA((6,)),
        ],
        compiler_params=PARAMS,
        name="forward",
    )(shot_data, point_store, point_slot.reshape(1, NS), taper_mask, recv_start.reshape(1, NS), band_tables()[0])


def run_product(got):
    return pl.pallas_call(
        product_kernel,
        out_shape=pltpu.VMEM((DEV, NS // 2, ROWS, 128), jnp.bfloat16),
        out_specs=pl.BlockSpec(memory_space=pltpu.VMEM),
        scratch_shapes=[
            pltpu.VMEM((7, (NS + 1) * PITCH, 128), jnp.float32),
            pltpu.VMEM((2, 512, 256), jnp.bfloat16),
            pltpu.VMEM((1024, 640), jnp.float32),
            pltpu.VMEM(((DEV + 1) * PITCH, 128), jnp.float32),
        ],
        compiler_params=PARAMS,
        name="product",
        in_specs=[pl.BlockSpec(memory_space=pltpu.VMEM)],
    )(pltpu.with_memory_space_constraint(got, pltpu.VMEM))


def run_inverse(back):
    vmem = lambda x: pltpu.with_memory_space_constraint(x, pltpu.VMEM)
    return pl.pallas_call(
        inverse_kernel,
        in_specs=[pl.BlockSpec(memory_space=pltpu.VMEM)] * 2,
        out_specs=pl.BlockSpec(memory_space=pl.ANY),
        out_shape=jax.ShapeDtypeStruct((NS, SHARE, NT), jnp.float32),
        scratch_shapes=[
            pltpu.VMEM((NS, SHARE, NT), jnp.float32),
            pltpu.SemaphoreType.DMA((NS // 2,)),
        ],
        compiler_params=PARAMS,
        name="inverse",
    )(vmem(back), vmem(band_tables()[1]))


def per_device(shot_data, point_store, point_slot, taper_mask, recv_start):
    sent = run_forward(shot_data, point_store, point_slot, taper_mask, recv_start)
    got = lax.all_to_all(sent, ("shot", "pt"), 0, 0, tiled=True)
    back = lax.all_to_all(run_product(got), ("shot", "pt"), 0, 0, tiled=True)
    return run_inverse(back)


def solution(mesh):
    placed = (
        P("shot", "pt", None),
        P(("shot", "pt"), None, None),
        P("pt"),
        P("shot", "pt"),
        P("shot"),
    )
    return jax.shard_map(
        per_device, mesh=mesh, in_specs=placed, out_specs=P("shot", "pt", None), check_vma=False
    )
```

```python
import functools
import math

import jax
import jax.numpy as jnp
import numpy as np
from jax import lax
from jax.experimental import pallas as pl
from jax.experimental.pallas import tpu as pltpu
from jax.sharding import PartitionSpec as P


NT = 1024
NF = 256
GRID = 576
SPREAD = 512
DEV = 128
ROWS = 4
NS = 16
NPT = 8
SHARE = 64
SHOTROWS = NS * NS
VMEM = 56 * 1024 * 1024
PITCH = 40


def band_tables():
    phase = (np.arange(NT)[:, None] * np.arange(NF)[None, :]) % NT
    angle = phase.astype(np.float32) * np.float32(2.0 * math.pi / NT)
    cosine = np.cos(angle).T
    sine = np.sin(angle).T
    weights = np.where(np.arange(NF) == 0, 1.0, 2.0).astype(np.float32)[:, None] / np.float32(NT)
    forward = np.stack([cosine, -sine], axis=1)
    inverse = np.stack([weights * cosine, -weights * sine], axis=1)
    forward = jnp.asarray(forward.reshape(ROWS * DEV, NT).T[: NT // 2], jnp.bfloat16)
    inverse = jnp.asarray(inverse.reshape(ROWS * DEV, NT), jnp.bfloat16)
    return forward, inverse


def iota(shape, dim):
    return lax.broadcasted_iota(jnp.int32, shape, dim)


def dot_nt(left, right):
    return lax.dot_general(left, right, (((1,), (1,)), ((), ())), preferred_element_type=jnp.float32)


def dot_nn(left, right):
    return jnp.dot(left, right, preferred_element_type=jnp.float32)


def order_matrix(slot_ref, mask_ref):
    f32, b16 = jnp.float32, jnp.bfloat16
    wide = NS * NS
    spread = (iota((NS, wide), 1) % NS == iota((NS, wide), 0)).astype(f32).astype(b16)
    owner = lax.shift_right_logical(slot_ref[...], 3).astype(f32).astype(b16)
    owner = dot_nn(jnp.broadcast_to(owner, (NS, NS)), spread)[0:1].astype(jnp.int32)
    taper = dot_nn(mask_ref[...].astype(f32).astype(b16), spread)
    taper = jnp.where(iota((NS, wide), 1) // NS == iota((NS, wide), 0), taper, 0.0)
    taper = jnp.sum(taper, axis=0, keepdims=True)
    r, l = iota((wide, wide), 0), iota((wide, wide), 1)
    return jnp.where((r // NS == l // NS) & (owner == r % NS), taper, 0.0).astype(b16)


def forward_kernel(
    shot_any, store_any, slot_any, mask_any, start_any, table_any, out_ref,
    shot, store, slot, mask, first, table, sems,
):
    f32, b16 = jnp.float32, jnp.bfloat16
    pairs = [(slot_any, slot), (mask_any, mask), (start_any, first), (table_any, table.at[pl.ds(0, NT // 2)])]
    pairs += [(shot_any, shot), (store_any.at[0], store)]
    loads = [pltpu.make_async_copy(src, dst, sems.at[n]) for n, (src, dst) in enumerate(pairs)]
    for load in loads:
        load.start()
    for load in loads[:3]:
        load.wait()
    order = order_matrix(slot, mask)
    start = jnp.broadcast_to(first[...].astype(f32).astype(b16), (NS, NS))
    start = jnp.where(iota((NS, NS), 0) == iota((NS, NS), 1), start, 0).astype(b16)
    start = dot_nn(start, jnp.ones((NS, ROWS * DEV), b16)).astype(b16)
    start = jnp.concatenate([start, jnp.zeros((64 - NS, ROWS * DEV), b16)], axis=0)
    loads[3].wait()
    sign = jnp.where(iota((1, ROWS * DEV), 1) % ROWS < 2, 1.0, -1.0).astype(b16)
    table[NT // 2 :] = table[: NT // 2] * sign
    loads[4].wait()
    spectra = dot_nn(shot[...].reshape(SHOTROWS, NT), table[...]).astype(b16)
    loads[5].wait()

    def put(block, value):
        for n in range(value.shape[0] // 128):
            out_ref[:, block + n] = value[128 * n : 128 * (n + 1)].T.reshape(DEV, ROWS, 128)

    put(2, jnp.concatenate([dot_nn(store[...], table[...]).astype(b16), start], axis=0))
    put(0, dot_nn(order, spectra).astype(b16))


def product_kernel(in_ref, out_ref, rows, left, prod, wins):
    f32, b16 = jnp.float32, jnp.bfloat16
    for block in range(7):
        for s in range(NS):
            part = in_ref[s * NPT : (s + 1) * NPT, block].astype(f32)
            rows[block, s * PITCH : s * PITCH + NPT * ROWS] = part.reshape(NPT * ROWS, 128)

    def piece(block, c, p):
        return rows[block, pl.ds(p * ROWS + c, NS, PITCH), :]

    arrived = jnp.concatenate(
        [piece(half, c, p) for p in range(NPT) for half in range(2) for c in range(ROWS)], axis=0
    ).astype(b16)
    place = (iota((NS, 128), 0) == iota((NS, 128), 1) % NS).astype(f32).astype(b16)
    zero = jnp.zeros((NS, 128), b16)
    own = (iota((8, 256), 1) % 128 // NS)[None]
    spectra = []
    for n in range(4):
        tile = [[place if s == 2 * n + m else zero for s in range(8)] for m in range(2)]
        tile = jnp.concatenate([jnp.concatenate(rows_of, axis=0) for rows_of in tile], axis=1)
        spread = dot_nn(arrived, tile).reshape(NPT, 16, 8, 256)
        chosen = spread[0]
        for p in range(1, NPT):
            chosen = jnp.where(own == p, spread[p], chosen)
        spectra.append(chosen.reshape(128, 256))

    def product(f):
        for s in range(NS):
            top = s // 8 * 64 + 2 * f * NS
            cols = slice(s % 2 * 128, (s % 2 + 1) * 128)
            part = spectra[s % 8 // 2]
            re, im = part[top : top + NS, cols], part[top + NS : top + 2 * NS, cols]
            left[f, s * NS : (s + 1) * NS, 0:128] = re.astype(b16)
            left[f, s * NS : (s + 1) * NS, 128:256] = (-im).astype(b16)
            left[f, 256 + s * NS : 256 + (s + 1) * NS, 0:128] = im.astype(b16)
            left[f, 256 + s * NS : 256 + (s + 1) * NS, 128:256] = re.astype(b16)
        for n, blocks in ((0, 2), (2, 2), (4, 1)):
            right = jnp.concatenate(
                [
                    jnp.concatenate([piece(2 + n + m, 2 * f + part, p) for m in range(blocks)], axis=1)
                    for part in range(2)
                    for p in range(NPT)
                ],
                axis=0,
            ).astype(b16)
            prod[f * 512 : (f + 1) * 512, 128 * n : 128 * (n + blocks)] = dot_nn(left[f], right)

    first = piece(6, 0, 0)[:, 64:80]
    lane = iota((NS, 128), 1)
    low = lane < 64

    def cut(f, pair):
        begin = [
            jnp.broadcast_to(first[:, 2 * pair + e : 2 * pair + e + 1], (NS, 128)).astype(jnp.int32) for e in range(2)
        ]
        at = [lane + begin[0], lane + begin[1] + 64]
        index = [x & 127 for x in at]
        here = [at[0] < 128, (lane >= 64) | (at[1] < 128)]
        for c in (2 * f, 2 * f + 1):
            base = c * 256 + 2 * pair * NS
            ahead = [None, None]
            for v in range(4, -1, -1):
                tiles = []
                for e in range(2):
                    src = prod[base + e * NS : base + (e + 1) * NS, 128 * v : 128 * (v + 1)]
                    turned = jnp.take_along_axis(src, index[e], axis=1)
                    if v < 4:
                        tiles.append(jnp.where(here[e], turned, ahead[e]))
                    ahead[e] = turned
                if v < 4:
                    slot = pair * ROWS + c
                    wins[pl.ds(2 * v * NS * PITCH + slot, NS, PITCH), :] = jnp.where(low, tiles[0], tiles[1])
                    wins[pl.ds((2 * v + 1) * NS * PITCH + slot, NS, PITCH), :] = jnp.where(low, tiles[1], tiles[0])

    product(0)
    product(1)
    for pair in range(8):
        cut(0, pair)
    for pair in range(8):
        cut(1, pair)
    for d in range(DEV):
        at = (d % NPT * NS + d // NPT) * PITCH
        out_ref[d] = wins[at : at + 32].reshape(NS // 2, ROWS, 128).astype(b16)


def inverse_kernel(in_ref, table_ref, out_any, result, sems):
    swap = lax.axis_index("pt") % 2
    copies = []
    for pair in range(NS // 2):
        left = in_ref[:, pair].reshape(DEV * ROWS, 128).T
        traces = dot_nn(left, table_ref[...])
        for e in range(2):
            result[2 * pair + (swap if e == 0 else 1 - swap)] = traces[e * SHARE : (e + 1) * SHARE]
        shots = pl.ds(2 * pair, 2)
        copies.append(pltpu.make_async_copy(result.at[shots], out_any.at[shots], sems.at[pair]))
        copies[-1].start()
    for copy in copies:
        copy.wait()


PARAMS = pltpu.CompilerParams(vmem_limit_bytes=VMEM)


def run_forward(shot_data, point_store, point_slot, taper_mask, recv_start):
    return pl.pallas_call(
        forward_kernel,
        out_shape=pltpu.VMEM((DEV, 7, ROWS, 128), jnp.bfloat16),
        out_specs=pl.BlockSpec(memory_space=pltpu.VMEM),
        in_specs=[pl.BlockSpec(memory_space=pl.ANY)] * 6,
        scratch_shapes=[
            pltpu.VMEM((NS, NS, NT), jnp.bfloat16),
            pltpu.VMEM((GRID, NT), jnp.bfloat16),
            pltpu.VMEM((1, NS), jnp.int32),
            pltpu.VMEM((NS, NS), jnp.int32),
            pltpu.VMEM((1, NS), jnp.int32),
            pltpu.VMEM((NT, ROWS * DEV), jnp.bfloat16),
            pltpu.SemaphoreType.DMA((6,)),
        ],
        compiler_params=PARAMS,
        name="forward",
    )(shot_data, point_store, point_slot.reshape(1, NS), taper_mask, recv_start.reshape(1, NS), band_tables()[0])


def run_product(got):
    return pl.pallas_call(
        product_kernel,
        out_shape=pltpu.VMEM((DEV, NS // 2, ROWS, 128), jnp.bfloat16),
        out_specs=pl.BlockSpec(memory_space=pltpu.VMEM),
        scratch_shapes=[
            pltpu.VMEM((7, (NS + 1) * PITCH, 128), jnp.float32),
            pltpu.VMEM((2, 512, 256), jnp.bfloat16),
            pltpu.VMEM((1024, 640), jnp.float32),
            pltpu.VMEM(((DEV + 1) * PITCH, 128), jnp.float32),
        ],
        compiler_params=PARAMS,
        name="product",
        in_specs=[pl.BlockSpec(memory_space=pltpu.VMEM)],
    )(pltpu.with_memory_space_constraint(got, pltpu.VMEM))


def run_inverse(back):
    vmem = lambda x: pltpu.with_memory_space_constraint(x, pltpu.VMEM)
    return pl.pallas_call(
        inverse_kernel,
        in_specs=[pl.BlockSpec(memory_space=pltpu.VMEM)] * 2,
        out_specs=pl.BlockSpec(memory_space=pl.ANY),
        out_shape=jax.ShapeDtypeStruct((NS, SHARE, NT), jnp.float32),
        scratch_shapes=[
            pltpu.VMEM((NS, SHARE, NT), jnp.float32),
            pltpu.SemaphoreType.DMA((NS // 2,)),
        ],
        compiler_params=PARAMS,
        name="inverse",
    )(vmem(back), vmem(band_tables()[1]))


def per_device(shot_data, point_store, point_slot, taper_mask, recv_start):
    sent = run_forward(shot_data, point_store, point_slot, taper_mask, recv_start)
    got = lax.all_to_all(sent, ("shot", "pt"), 0, 0, tiled=True)
    back = lax.all_to_all(run_product(got), ("shot", "pt"), 0, 0, tiled=True)
    return run_inverse(back)


def solution(mesh):
    placed = (
        P("shot", "pt", None),
        P(("shot", "pt"), None, None),
        P("pt"),
        P("shot", "pt"),
        P("shot"),
    )
    return jax.shard_map(
        per_device, mesh=mesh, in_specs=placed, out_specs=P("shot", "pt", None), check_vma=False
    )
```

```python
import functools
import math

import jax
import jax.numpy as jnp
import numpy as np
from jax import lax
from jax.experimental import pallas as pl
from jax.experimental.pallas import tpu as pltpu
from jax.sharding import PartitionSpec as P


NT = 1024
NF = 256
GRID = 576
SPREAD = 512
DEV = 128
ROWS = 4
NS = 16
NPT = 8
SHARE = 64
SHOTROWS = NS * NS
VMEM = 56 * 1024 * 1024
PITCH = 40


def band_tables():
    phase = (np.arange(NT)[:, None] * np.arange(NF)[None, :]) % NT
    angle = phase.astype(np.float32) * np.float32(2.0 * math.pi / NT)
    cosine = np.cos(angle).T
    sine = np.sin(angle).T
    weights = np.where(np.arange(NF) == 0, 1.0, 2.0).astype(np.float32)[:, None] / np.float32(NT)
    forward = np.stack([cosine, -sine], axis=1)
    inverse = np.stack([weights * cosine, -weights * sine], axis=1)
    forward = jnp.asarray(forward.reshape(ROWS * DEV, NT).T[: NT // 2], jnp.bfloat16)
    inverse = jnp.asarray(inverse.reshape(ROWS * DEV, NT), jnp.bfloat16)
    return forward, inverse


def iota(shape, dim):
    return lax.broadcasted_iota(jnp.int32, shape, dim)


def dot_nt(left, right):
    return lax.dot_general(left, right, (((1,), (1,)), ((), ())), preferred_element_type=jnp.float32)


def dot_nn(left, right):
    return jnp.dot(left, right, preferred_element_type=jnp.float32)


def order_matrix(slot_ref, mask_ref):
    f32, b16 = jnp.float32, jnp.bfloat16
    wide = NS * NS
    spread = (iota((NS, wide), 1) % NS == iota((NS, wide), 0)).astype(f32).astype(b16)
    owner = lax.shift_right_logical(slot_ref[...], 3).astype(f32).astype(b16)
    owner = dot_nn(jnp.broadcast_to(owner, (NS, NS)), spread)[0:1].astype(jnp.int32)
    taper = dot_nn(mask_ref[...].astype(f32).astype(b16), spread)
    taper = jnp.where(iota((NS, wide), 1) // NS == iota((NS, wide), 0), taper, 0.0)
    taper = jnp.sum(taper, axis=0, keepdims=True)
    r, l = iota((wide, wide), 0), iota((wide, wide), 1)
    return jnp.where((r // NS == l // NS) & (owner == r % NS), taper, 0.0).astype(b16)


def forward_kernel(
    shot_any, store_any, slot_any, mask_any, start_any, table_any, out_ref,
    shot, store, slot, mask, first, table, sems,
):
    f32, b16 = jnp.float32, jnp.bfloat16
    pairs = [(slot_any, slot), (mask_any, mask), (start_any, first), (table_any, table.at[pl.ds(0, NT // 2)])]
    pairs += [(shot_any, shot), (store_any.at[0], store)]
    loads = [pltpu.make_async_copy(src, dst, sems.at[n]) for n, (src, dst) in enumerate(pairs)]
    for load in loads:
        load.start()
    for load in loads[:3]:
        load.wait()
    order = order_matrix(slot, mask)
    start = jnp.broadcast_to(first[...].astype(f32).astype(b16), (NS, NS))
    start = jnp.where(iota((NS, NS), 0) == iota((NS, NS), 1), start, 0).astype(b16)
    start = dot_nn(start, jnp.ones((NS, ROWS * DEV), b16)).astype(b16)
    start = jnp.concatenate([start, jnp.zeros((64 - NS, ROWS * DEV), b16)], axis=0)
    loads[3].wait()
    loads[4].wait()
    sign = jnp.where(iota((1, ROWS * DEV), 1) % ROWS < 2, 1.0, -1.0).astype(b16)
    table[NT // 2 :] = table[: NT // 2] * sign
    spectra = dot_nn(shot[...].reshape(SHOTROWS, NT), table[...]).astype(b16)
    loads[5].wait()

    def put(block, value):
        for n in range(value.shape[0] // 128):
            out_ref[:, block + n] = value[128 * n : 128 * (n + 1)].T.reshape(DEV, ROWS, 128)

    put(2, jnp.concatenate([dot_nn(store[...], table[...]).astype(b16), start], axis=0))
    put(0, dot_nn(order, spectra).astype(b16))


def product_kernel(in_ref, out_ref, rows, left, prod, wins):
    f32, b16 = jnp.float32, jnp.bfloat16
    for block in range(7):
        for s in range(NS):
            part = in_ref[s * NPT : (s + 1) * NPT, block].astype(f32)
            rows[block, s * PITCH : s * PITCH + NPT * ROWS] = part.reshape(NPT * ROWS, 128)

    def piece(block, c, p):
        return rows[block, pl.ds(p * ROWS + c, NS, PITCH), :]

    arrived = jnp.concatenate(
        [piece(half, c, p) for p in range(NPT) for half in range(2) for c in range(ROWS)], axis=0
    ).astype(b16)
    place = (iota((NS, 128), 0) == iota((NS, 128), 1) % NS).astype(f32).astype(b16)
    zero = jnp.zeros((NS, 128), b16)
    own = (iota((8, 256), 1) % 128 // NS)[None]
    spectra = []
    for n in range(4):
        tile = [[place if s == 2 * n + m else zero for s in range(8)] for m in range(2)]
        tile = jnp.concatenate([jnp.concatenate(rows_of, axis=0) for rows_of in tile], axis=1)
        spread = dot_nn(arrived, tile).reshape(NPT, 16, 8, 256)
        chosen = spread[0]
        for p in range(1, NPT):
            chosen = jnp.where(own == p, spread[p], chosen)
        spectra.append(chosen.reshape(128, 256))

    def product(f):
        for s in range(NS):
            top = s // 8 * 64 + 2 * f * NS
            cols = slice(s % 2 * 128, (s % 2 + 1) * 128)
            part = spectra[s % 8 // 2]
            re, im = part[top : top + NS, cols], part[top + NS : top + 2 * NS, cols]
            left[f, s * NS : (s + 1) * NS, 0:128] = re.astype(b16)
            left[f, s * NS : (s + 1) * NS, 128:256] = (-im).astype(b16)
            left[f, 256 + s * NS : 256 + (s + 1) * NS, 0:128] = im.astype(b16)
            left[f, 256 + s * NS : 256 + (s + 1) * NS, 128:256] = re.astype(b16)
        for n, blocks in ((0, 2), (2, 2), (4, 1)):
            right = jnp.concatenate(
                [
                    jnp.concatenate([piece(2 + n + m, 2 * f + part, p) for m in range(blocks)], axis=1)
                    for part in range(2)
                    for p in range(NPT)
                ],
                axis=0,
            ).astype(b16)
            prod[f * 512 : (f + 1) * 512, 128 * n : 128 * (n + blocks)] = dot_nn(left[f], right)

    first = piece(6, 0, 0)[:, 64:80]
    lane = iota((NS, 128), 1)
    low = lane < 64

    def cut(f, pair):
        begin = [
            jnp.broadcast_to(first[:, 2 * pair + e : 2 * pair + e + 1], (NS, 128)).astype(jnp.int32) for e in range(2)
        ]
        at = [lane + begin[0], lane + begin[1] + 64]
        index = [x & 127 for x in at]
        here = [at[0] < 128, (lane >= 64) | (at[1] < 128)]
        for c in (2 * f, 2 * f + 1):
            base = c * 256 + 2 * pair * NS
            ahead = [None, None]
            for v in range(4, -1, -1):
                tiles = []
                for e in range(2):
                    src = prod[base + e * NS : base + (e + 1) * NS, 128 * v : 128 * (v + 1)]
                    turned = jnp.take_along_axis(src, index[e], axis=1)
                    if v < 4:
                        tiles.append(jnp.where(here[e], turned, ahead[e]))
                    ahead[e] = turned
                if v < 4:
                    slot = pair * ROWS + c
                    wins[pl.ds(2 * v * NS * PITCH + slot, NS, PITCH), :] = jnp.where(low, tiles[0], tiles[1])
                    wins[pl.ds((2 * v + 1) * NS * PITCH + slot, NS, PITCH), :] = jnp.where(low, tiles[1], tiles[0])

    product(0)
    product(1)
    for pair in range(8):
        cut(0, pair)
    for pair in range(8):
        cut(1, pair)
    for d in range(DEV):
        at = (d % NPT * NS + d // NPT) * PITCH
        out_ref[d] = wins[at : at + 32].reshape(NS // 2, ROWS, 128).astype(b16)


def inverse_kernel(in_ref, table_ref, out_any, result, sems):
    swap = lax.axis_index("pt") % 2
    copies = []
    for pair in range(NS // 2):
        left = in_ref[:, pair].reshape(DEV * ROWS, 128).T
        traces = dot_nn(left, table_ref[...])
        for e in range(2):
            result[2 * pair + (swap if e == 0 else 1 - swap)] = traces[e * SHARE : (e + 1) * SHARE]
        shots = pl.ds(2 * pair, 2)
        copies.append(pltpu.make_async_copy(result.at[shots], out_any.at[shots], sems.at[pair]))
        copies[-1].start()
    for copy in copies:
        copy.wait()


PARAMS = pltpu.CompilerParams(vmem_limit_bytes=VMEM)


def run_forward(shot_data, point_store, point_slot, taper_mask, recv_start):
    return pl.pallas_call(
        forward_kernel,
        out_shape=pltpu.VMEM((DEV, 7, ROWS, 128), jnp.bfloat16),
        out_specs=pl.BlockSpec(memory_space=pltpu.VMEM),
        in_specs=[pl.BlockSpec(memory_space=pl.ANY)] * 6,
        scratch_shapes=[
            pltpu.VMEM((NS, NS, NT), jnp.bfloat16),
            pltpu.VMEM((GRID, NT), jnp.bfloat16),
            pltpu.VMEM((1, NS), jnp.int32),
            pltpu.VMEM((NS, NS), jnp.int32),
            pltpu.VMEM((1, NS), jnp.int32),
            pltpu.VMEM((NT, ROWS * DEV), jnp.bfloat16),
            pltpu.SemaphoreType.DMA((6,)),
        ],
        compiler_params=PARAMS,
        name="forward",
    )(shot_data, point_store, point_slot.reshape(1, NS), taper_mask, recv_start.reshape(1, NS), band_tables()[0])


def run_product(got):
    return pl.pallas_call(
        product_kernel,
        out_shape=pltpu.VMEM((DEV, NS // 2, ROWS, 128), jnp.bfloat16),
        out_specs=pl.BlockSpec(memory_space=pltpu.VMEM),
        scratch_shapes=[
            pltpu.VMEM((7, (NS + 1) * PITCH, 128), jnp.float32),
            pltpu.VMEM((2, 512, 256), jnp.bfloat16),
            pltpu.VMEM((1024, 640), jnp.float32),
            pltpu.VMEM(((DEV + 1) * PITCH, 128), jnp.float32),
        ],
        compiler_params=PARAMS,
        name="product",
        in_specs=[pl.BlockSpec(memory_space=pltpu.VMEM)],
    )(pltpu.with_memory_space_constraint(got, pltpu.VMEM))


def run_inverse(back):
    vmem = lambda x: pltpu.with_memory_space_constraint(x, pltpu.VMEM)
    return pl.pallas_call(
        inverse_kernel,
        in_specs=[pl.BlockSpec(memory_space=pltpu.VMEM)] * 2,
        out_specs=pl.BlockSpec(memory_space=pl.ANY),
        out_shape=jax.ShapeDtypeStruct((NS, SHARE, NT), jnp.float32),
        scratch_shapes=[
            pltpu.VMEM((NS, SHARE, NT), jnp.float32),
            pltpu.SemaphoreType.DMA((NS // 2,)),
        ],
        compiler_params=PARAMS,
        name="inverse",
    )(vmem(back), vmem(band_tables()[1]))


def per_device(shot_data, point_store, point_slot, taper_mask, recv_start):
    sent = run_forward(shot_data, point_store, point_slot, taper_mask, recv_start)
    got = lax.all_to_all(sent, ("shot", "pt"), 0, 0, tiled=True)
    back = lax.all_to_all(run_product(got), ("shot", "pt"), 0, 0, tiled=True)
    return run_inverse(back)


def solution(mesh):
    placed = (
        P("shot", "pt", None),
        P(("shot", "pt"), None, None),
        P("pt"),
        P("shot", "pt"),
        P("shot"),
    )
    return jax.shard_map(
        per_device, mesh=mesh, in_specs=placed, out_specs=P("shot", "pt", None), check_vma=False
    )
```

```python
import functools
import math

import jax
import jax.numpy as jnp
import numpy as np
from jax import lax
from jax.experimental import pallas as pl
from jax.experimental.pallas import tpu as pltpu
from jax.sharding import PartitionSpec as P


NT = 1024
NF = 256
GRID = 576
SPREAD = 512
DEV = 128
ROWS = 4
NS = 16
NPT = 8
SHARE = 64
SHOTROWS = NS * NS
VMEM = 56 * 1024 * 1024
PITCH = 40


def band_tables():
    phase = (np.arange(NT)[:, None] * np.arange(NF)[None, :]) % NT
    angle = phase.astype(np.float32) * np.float32(2.0 * math.pi / NT)
    cosine = np.cos(angle).T
    sine = np.sin(angle).T
    weights = np.where(np.arange(NF) == 0, 1.0, 2.0).astype(np.float32)[:, None] / np.float32(NT)
    forward = np.stack([cosine, -sine], axis=1)
    inverse = np.stack([weights * cosine, -weights * sine], axis=1)
    forward = jnp.asarray(forward.reshape(ROWS * DEV, NT).T[: NT // 2], jnp.bfloat16)
    inverse = jnp.asarray(inverse.reshape(ROWS * DEV, NT), jnp.bfloat16)
    return forward, inverse


def iota(shape, dim):
    return lax.broadcasted_iota(jnp.int32, shape, dim)


def dot_nt(left, right):
    return lax.dot_general(left, right, (((1,), (1,)), ((), ())), preferred_element_type=jnp.float32)


def dot_nn(left, right):
    return jnp.dot(left, right, preferred_element_type=jnp.float32)


def order_matrix(slot_ref, mask_ref):
    f32, b16 = jnp.float32, jnp.bfloat16
    wide = NS * NS
    spread = (iota((NS, wide), 1) % NS == iota((NS, wide), 0)).astype(f32).astype(b16)
    owner = lax.shift_right_logical(slot_ref[...], 3).astype(f32).astype(b16)
    owner = dot_nn(jnp.broadcast_to(owner, (NS, NS)), spread)[0:1].astype(jnp.int32)
    taper = dot_nn(mask_ref[...].astype(f32).astype(b16), spread)
    taper = jnp.where(iota((NS, wide), 1) // NS == iota((NS, wide), 0), taper, 0.0)
    taper = jnp.sum(taper, axis=0, keepdims=True)
    r, l = iota((wide, wide), 0), iota((wide, wide), 1)
    return jnp.where((r // NS == l // NS) & (owner == r % NS), taper, 0.0).astype(b16)


def forward_kernel(
    shot_any, store_any, slot_any, mask_any, start_any, table_any, out_ref,
    shot, store, slot, mask, first, table, sems,
):
    f32, b16 = jnp.float32, jnp.bfloat16
    pairs = [(slot_any, slot), (mask_any, mask), (start_any, first), (table_any, table.at[pl.ds(0, NT // 2)])]
    pairs += [(shot_any, shot), (store_any.at[0], store)]
    loads = [pltpu.make_async_copy(src, dst, sems.at[n]) for n, (src, dst) in enumerate(pairs)]
    for n in (3, 4, 0, 1, 2, 5):
        loads[n].start()
    for load in loads[:3]:
        load.wait()
    order = order_matrix(slot, mask)
    start = jnp.broadcast_to(first[...].astype(f32).astype(b16), (NS, NS))
    start = jnp.where(iota((NS, NS), 0) == iota((NS, NS), 1), start, 0).astype(b16)
    start = dot_nn(start, jnp.ones((NS, ROWS * DEV), b16)).astype(b16)
    start = jnp.concatenate([start, jnp.zeros((64 - NS, ROWS * DEV), b16)], axis=0)
    loads[3].wait()
    loads[4].wait()
    sign = jnp.where(iota((1, ROWS * DEV), 1) % ROWS < 2, 1.0, -1.0).astype(b16)
    table[NT // 2 :] = table[: NT // 2] * sign
    spectra = dot_nn(shot[...].reshape(SHOTROWS, NT), table[...]).astype(b16)
    loads[5].wait()

    def put(block, value):
        for n in range(value.shape[0] // 128):
            out_ref[:, block + n] = value[128 * n : 128 * (n + 1)].T.reshape(DEV, ROWS, 128)

    put(2, jnp.concatenate([dot_nn(store[...], table[...]).astype(b16), start], axis=0))
    put(0, dot_nn(order, spectra).astype(b16))


def product_kernel(in_ref, out_ref, rows, left, prod, wins):
    f32, b16 = jnp.float32, jnp.bfloat16
    for block in range(7):
        for s in range(NS):
            part = in_ref[s * NPT : (s + 1) * NPT, block].astype(f32)
            rows[block, s * PITCH : s * PITCH + NPT * ROWS] = part.reshape(NPT * ROWS, 128)

    def piece(block, c, p):
        return rows[block, pl.ds(p * ROWS + c, NS, PITCH), :]

    arrived = jnp.concatenate(
        [piece(half, c, p) for p in range(NPT) for half in range(2) for c in range(ROWS)], axis=0
    ).astype(b16)
    place = (iota((NS, 128), 0) == iota((NS, 128), 1) % NS).astype(f32).astype(b16)
    zero = jnp.zeros((NS, 128), b16)
    own = (iota((8, 256), 1) % 128 // NS)[None]
    spectra = []
    for n in range(4):
        tile = [[place if s == 2 * n + m else zero for s in range(8)] for m in range(2)]
        tile = jnp.concatenate([jnp.concatenate(rows_of, axis=0) for rows_of in tile], axis=1)
        spread = dot_nn(arrived, tile).reshape(NPT, 16, 8, 256)
        chosen = spread[0]
        for p in range(1, NPT):
            chosen = jnp.where(own == p, spread[p], chosen)
        spectra.append(chosen.reshape(128, 256))

    def product(f):
        for s in range(NS):
            top = s // 8 * 64 + 2 * f * NS
            cols = slice(s % 2 * 128, (s % 2 + 1) * 128)
            part = spectra[s % 8 // 2]
            re, im = part[top : top + NS, cols], part[top + NS : top + 2 * NS, cols]
            left[f, s * NS : (s + 1) * NS, 0:128] = re.astype(b16)
            left[f, s * NS : (s + 1) * NS, 128:256] = (-im).astype(b16)
            left[f, 256 + s * NS : 256 + (s + 1) * NS, 0:128] = im.astype(b16)
            left[f, 256 + s * NS : 256 + (s + 1) * NS, 128:256] = re.astype(b16)
        for n, blocks in ((0, 2), (2, 2), (4, 1)):
            right = jnp.concatenate(
                [
                    jnp.concatenate([piece(2 + n + m, 2 * f + part, p) for m in range(blocks)], axis=1)
                    for part in range(2)
                    for p in range(NPT)
                ],
                axis=0,
            ).astype(b16)
            prod[f * 512 : (f + 1) * 512, 128 * n : 128 * (n + blocks)] = dot_nn(left[f], right)

    first = piece(6, 0, 0)[:, 64:80]
    lane = iota((NS, 128), 1)
    low = lane < 64

    def cut(f, pair):
        begin = [
            jnp.broadcast_to(first[:, 2 * pair + e : 2 * pair + e + 1], (NS, 128)).astype(jnp.int32) for e in range(2)
        ]
        at = [lane + begin[0], lane + begin[1] + 64]
        index = [x & 127 for x in at]
        here = [at[0] < 128, (lane >= 64) | (at[1] < 128)]
        for c in (2 * f, 2 * f + 1):
            base = c * 256 + 2 * pair * NS
            ahead = [None, None]
            for v in range(4, -1, -1):
                tiles = []
                for e in range(2):
                    src = prod[base + e * NS : base + (e + 1) * NS, 128 * v : 128 * (v + 1)]
                    turned = jnp.take_along_axis(src, index[e], axis=1)
                    if v < 4:
                        tiles.append(jnp.where(here[e], turned, ahead[e]))
                    ahead[e] = turned
                if v < 4:
                    slot = pair * ROWS + c
                    wins[pl.ds(2 * v * NS * PITCH + slot, NS, PITCH), :] = jnp.where(low, tiles[0], tiles[1])
                    wins[pl.ds((2 * v + 1) * NS * PITCH + slot, NS, PITCH), :] = jnp.where(low, tiles[1], tiles[0])

    product(0)
    product(1)
    for pair in range(8):
        cut(0, pair)
    for pair in range(8):
        cut(1, pair)
    for d in range(DEV):
        at = (d % NPT * NS + d // NPT) * PITCH
        out_ref[d] = wins[at : at + 32].reshape(NS // 2, ROWS, 128).astype(b16)


def inverse_kernel(in_ref, table_ref, out_any, result, sems):
    swap = lax.axis_index("pt") % 2
    copies = []
    for pair in range(NS // 2):
        left = in_ref[:, pair].reshape(DEV * ROWS, 128).T
        traces = dot_nn(left, table_ref[...])
        for e in range(2):
            result[2 * pair + (swap if e == 0 else 1 - swap)] = traces[e * SHARE : (e + 1) * SHARE]
        shots = pl.ds(2 * pair, 2)
        copies.append(pltpu.make_async_copy(result.at[shots], out_any.at[shots], sems.at[pair]))
        copies[-1].start()
    for copy in copies:
        copy.wait()


PARAMS = pltpu.CompilerParams(vmem_limit_bytes=VMEM)


def run_forward(shot_data, point_store, point_slot, taper_mask, recv_start):
    return pl.pallas_call(
        forward_kernel,
        out_shape=pltpu.VMEM((DEV, 7, ROWS, 128), jnp.bfloat16),
        out_specs=pl.BlockSpec(memory_space=pltpu.VMEM),
        in_specs=[pl.BlockSpec(memory_space=pl.ANY)] * 6,
        scratch_shapes=[
            pltpu.VMEM((NS, NS, NT), jnp.bfloat16),
            pltpu.VMEM((GRID, NT), jnp.bfloat16),
            pltpu.VMEM((1, NS), jnp.int32),
            pltpu.VMEM((NS, NS), jnp.int32),
            pltpu.VMEM((1, NS), jnp.int32),
            pltpu.VMEM((NT, ROWS * DEV), jnp.bfloat16),
            pltpu.SemaphoreType.DMA((6,)),
        ],
        compiler_params=PARAMS,
        name="forward",
    )(shot_data, point_store, point_slot.reshape(1, NS), taper_mask, recv_start.reshape(1, NS), band_tables()[0])


def run_product(got):
    return pl.pallas_call(
        product_kernel,
        out_shape=pltpu.VMEM((DEV, NS // 2, ROWS, 128), jnp.bfloat16),
        out_specs=pl.BlockSpec(memory_space=pltpu.VMEM),
        scratch_shapes=[
            pltpu.VMEM((7, (NS + 1) * PITCH, 128), jnp.float32),
            pltpu.VMEM((2, 512, 256), jnp.bfloat16),
            pltpu.VMEM((1024, 640), jnp.float32),
            pltpu.VMEM(((DEV + 1) * PITCH, 128), jnp.float32),
        ],
        compiler_params=PARAMS,
        name="product",
        in_specs=[pl.BlockSpec(memory_space=pltpu.VMEM)],
    )(pltpu.with_memory_space_constraint(got, pltpu.VMEM))


def run_inverse(back):
    vmem = lambda x: pltpu.with_memory_space_constraint(x, pltpu.VMEM)
    return pl.pallas_call(
        inverse_kernel,
        in_specs=[pl.BlockSpec(memory_space=pltpu.VMEM)] * 2,
        out_specs=pl.BlockSpec(memory_space=pl.ANY),
        out_shape=jax.ShapeDtypeStruct((NS, SHARE, NT), jnp.float32),
        scratch_shapes=[
            pltpu.VMEM((NS, SHARE, NT), jnp.float32),
            pltpu.SemaphoreType.DMA((NS // 2,)),
        ],
        compiler_params=PARAMS,
        name="inverse",
    )(vmem(back), vmem(band_tables()[1]))


def per_device(shot_data, point_store, point_slot, taper_mask, recv_start):
    sent = run_forward(shot_data, point_store, point_slot, taper_mask, recv_start)
    got = lax.all_to_all(sent, ("shot", "pt"), 0, 0, tiled=True)
    back = lax.all_to_all(run_product(got), ("shot", "pt"), 0, 0, tiled=True)
    return run_inverse(back)


def solution(mesh):
    placed = (
        P("shot", "pt", None),
        P(("shot", "pt"), None, None),
        P("pt"),
        P("shot", "pt"),
        P("shot"),
    )
    return jax.shard_map(
        per_device, mesh=mesh, in_specs=placed, out_specs=P("shot", "pt", None), check_vma=False
    )
```
